32 devices in a mesh: gx: 4 (over z), gy: 8 (over y, x, core).
Axes of the slice: x: 2, y: 2, z: 4, core: 2. Of those that a mesh axis runs over, the one named last changes fastest.
Arguments:
- image: float32 [64, 256, 256], P('gx', 'gy'), may hold values from -6 to 6
- phases: int32 [64, 256, 256], P('gx', 'gy'), may hold values from 0 to 2
- phase_table: float32 [2, 3], replicated, may hold values from 0.2 to 8
- start_potential: float32 [64, 256, 256], P('gx', 'gy'), may hold values from 0 to 1
Outputs:
- conductivity: float32 [64, 256, 256], P('gx', 'gy')
- potential: float32 [64, 256, 256], P('gx', 'gy')
The draws below stay inside these ranges and needn't reach their ends.
Inputs may be any that keep to these rules, and one draw needn't show every extreme that they name: `phases`: 0 fibre, 1 binder, 2 pore.
All inputs are finite; a program needn't handle non-finite values.
Results may differ from the reference program's by a relative error of at most 0.00005.
Values sent between devices are 32-bit elements; how exact they have to be, the bound alone decides.
A program may use at most 128 MiB of HBM per device.

```python
import math
import jax
import jax.numpy as jnp

BX = 16
BY = 32
Z = 256
SWEEPS = 3
PHASES = 3
NX = 64
NY = 256


def edge_cells(key, length, brick):
    count = length // brick
    offsets = jax.random.randint(key, (count,), -6, 7)
    edges = jnp.arange(count, dtype=jnp.int32) * brick + offsets.astype(jnp.int32)
    positions = jnp.arange(length, dtype=jnp.int32)
    beyond = (positions[:, None] >= edges[None, 1:]).astype(jnp.int32)
    return jnp.sum(beyond, axis=1).astype(jnp.int32)


def draw_image(key, part):
    keys = jax.random.split(key, 10)
    cell_x = edge_cells(keys[0], NX, BX)
    cell_y = edge_cells(keys[1], NY, BY)
    count_x = NX // BX
    count_y = NY // BY
    loud = jax.random.uniform(keys[2], (count_x, count_y), jnp.float32, 1.7, 2.0)
    quiet = jax.random.uniform(keys[3], (count_x, count_y), jnp.float32, 0.1, 0.4)
    fibre_amp = 3.3
    wave = jax.random.uniform(keys[4], (), jnp.float32, 0.9, 1.1)
    noise = 0.2 * jnp.clip(jax.random.normal(keys[5], (NX, NY, Z), jnp.float32), -3.0, 3.0)
    angle = jax.random.uniform(keys[6], (), jnp.float32, 0.0, math.pi)
    fibre_phase = jax.random.uniform(keys[7], (), jnp.float32, -math.pi, math.pi)
    layer_freq = jax.random.uniform(keys[8], (), jnp.float32, 0.494, 0.5)
    cell_phase = jax.random.uniform(keys[9], (count_x, count_y), jnp.float32, -math.pi, math.pi)
    loud_cells = jnp.take(jnp.take(loud, cell_x, axis=0), cell_y, axis=1)
    quiet_cells = jnp.take(jnp.take(quiet, cell_x, axis=0), cell_y, axis=1)
    phase_cells = jnp.take(jnp.take(cell_phase, cell_x, axis=0), cell_y, axis=1)
    checker = (cell_x[:, None] + cell_y[None, :]) % 2 == 0
    level = jnp.where(checker, loud_cells, quiet_cells)
    pos_x = jnp.arange(NX, dtype=jnp.int32).astype(jnp.float32)
    pos_y = jnp.arange(NY, dtype=jnp.int32).astype(jnp.float32)
    pos_z = jnp.arange(Z, dtype=jnp.int32).astype(jnp.float32)
    fibre = fibre_amp * jnp.sin(wave * (pos_x[:, None] * jnp.cos(angle) + pos_y[None, :] * jnp.sin(angle)) + fibre_phase)
    layers = level[:, :, None] * jnp.sin(layer_freq * pos_z[None, None, :] + phase_cells[:, :, None])
    return (noise + fibre[:, :, None] + layers).astype(jnp.float32)


def draw_phase_table(key, part):
    keys = jax.random.split(key, 2)
    base = jnp.exp(jax.random.uniform(keys[0], (1, PHASES), jnp.float32, math.log(0.2), math.log(2.0)))
    aniso = jnp.exp(jax.random.uniform(keys[1], (1, PHASES), jnp.float32, math.log(4.0), math.log(8.0)))
    return jnp.concatenate([base, aniso], axis=0).astype(jnp.float32)


def with_ends(values, own_key, least, largest):
    extent = values.shape
    place = [jax.random.randint(jax.random.fold_in(own_key, axis), (), 0, extent[axis]) for axis in range(len(extent))]
    values = values.at[tuple(place)].set(least)
    longest = extent.index(max(extent))
    place[longest] = (place[longest] + 1) % extent[longest]
    return values.at[tuple(place)].set(largest)


def shard_levels(key, shape, cuts, least, high):
    def one(position, blocks):
        steps = jax.random.uniform(jax.random.fold_in(jax.random.fold_in(key, 6), position), (blocks,), jnp.float32, least / len(cuts), high / len(cuts))
        return jnp.repeat(jnp.exp(steps), shape[position] // blocks).reshape((-1,) + (1,) * (len(shape) - position - 1))

    gain = one(*cuts[0])
    for cut in cuts[1:]:
        gain = gain * one(*cut)
    return gain


def setup_inputs(seed: int = 0) -> dict:
    streams_of = jax.random.split(jax.random.key(seed), 5)
    return {
        "image": draw_image(jax.random.fold_in(streams_of[4], 71), 0),
        "phases": with_ends(jax.random.randint(streams_of[1], (NX, NY, Z), 0, 3), jax.random.fold_in(streams_of[1], 1), 0, 2).astype(jnp.int32),
        "phase_table": draw_phase_table(jax.random.fold_in(streams_of[4], 71), 0),
        "start_potential": jnp.clip(1.0 * jax.random.uniform(streams_of[3], (NX, NY, Z), jnp.float32) ** shard_levels(streams_of[3], (NX, NY, Z), ((0, 4), (1, 8)), -0.2, 0.2), 0.0, 1.0),
    }


def gauss_taps(sigma, reach, order):
    values = [math.exp(-offset * offset / (2.0 * sigma * sigma)) for offset in range(-reach, reach + 1)]
    total = sum(values)
    values = [value / total for value in values]
    if order == 1:
        values = [(index - reach) * values[index] / (sigma * sigma) for index in range(2 * reach + 1)]
    return values


def filter_dim(field, axis_number, taps):
    reach = (len(taps) - 1) // 2
    widths = [(0, 0), (0, 0), (0, 0)]
    widths[axis_number] = (reach, reach)
    padded = jnp.pad(field, widths)
    length = field.shape[axis_number]
    total = jnp.zeros(field.shape, jnp.float32)
    for offset in range(2 * reach + 1):
        piece = jnp.take(padded, jnp.arange(offset, offset + length, dtype=jnp.int32), axis=axis_number)
        total = total + float(taps[offset]) * piece
    return total


def harmonic(first, second):
    return 2.0 * first * second / (first + second)


def reference(image, phases, phase_table, start_potential):
    near_taps = gauss_taps(1.0, 3, 0)
    slope_taps = gauss_taps(1.0, 3, 1)
    wide_taps = gauss_taps(4.0, 12, 0)
    along = filter_dim(image, 2, near_taps)
    slope = filter_dim(image, 2, slope_taps)
    grad_x = filter_dim(filter_dim(along, 1, near_taps), 0, slope_taps)
    grad_y = filter_dim(filter_dim(along, 1, slope_taps), 0, near_taps)
    grad_z = filter_dim(filter_dim(slope, 1, near_taps), 0, near_taps)

    def smooth(field):
        return filter_dim(filter_dim(filter_dim(field, 2, wide_taps), 1, wide_taps), 0, wide_taps)

    jxx = smooth(grad_x * grad_x)
    jyy = smooth(grad_y * grad_y)
    jzz = smooth(grad_z * grad_z)
    jxy = smooth(grad_x * grad_y)
    jxz = smooth(grad_x * grad_z)
    jyz = smooth(grad_y * grad_z)
    trace = jxx + jyy + jzz
    shift = 0.1 * trace + 1e-6
    first = jxx + shift
    second = jyy + shift
    third = jzz + shift
    cof = first * second - jxy * jxy
    det = first * (second * third - jyz * jyz) - jxy * (jxy * third - jyz * jxz) + jxz * (jxy * jyz - second * jxz)
    weight = trace * cof / det
    conductivity = phase_table[0][phases] + 0.1 * phase_table[1][phases] * weight

    cond_pad = jnp.pad(conductivity, ((1, 1), (1, 1), (0, 0)))
    centre = conductivity
    coef_x0 = harmonic(centre, cond_pad[:-2, 1:-1])
    coef_x1 = harmonic(centre, cond_pad[2:, 1:-1])
    coef_y0 = harmonic(centre, cond_pad[1:-1, :-2])
    coef_y1 = harmonic(centre, cond_pad[1:-1, 2:])
    below = jnp.concatenate([centre[:, :, :1], centre[:, :, :-1]], axis=2)
    above = jnp.concatenate([centre[:, :, 1:], centre[:, :, -1:]], axis=2)
    coef_z0 = harmonic(centre, below)
    coef_z1 = harmonic(centre, above)
    denom = coef_x0 + coef_x1 + coef_y0 + coef_y1 + coef_z0 + coef_z1
    potential = start_potential
    for sweep_index in range(SWEEPS):
        pot_pad = jnp.pad(potential, ((1, 1), (1, 1), (0, 0)))
        pot_below = jnp.concatenate([jnp.ones_like(potential[:, :, :1]), potential[:, :, :-1]], axis=2)
        pot_above = jnp.concatenate([potential[:, :, 1:], jnp.zeros_like(potential[:, :, :1])], axis=2)
        numer = coef_x0 * pot_pad[:-2, 1:-1] + coef_x1 * pot_pad[2:, 1:-1]
        numer = numer + coef_y0 * pot_pad[1:-1, :-2] + coef_y1 * pot_pad[1:-1, 2:]
        numer = numer + coef_z0 * pot_below + coef_z1 * pot_above
        potential = numer / denom
    return conductivity, potential
```

```python
import functools
import math

import jax
import jax.numpy as jnp
import ml_dtypes
import numpy as np
from jax import lax
from jax.experimental import pallas as pl
from jax.experimental.pallas import tpu as pltpu
from jax.sharding import PartitionSpec as P

SWEEPS = 3
PHASES = 3
DERIV = 3
SMOOTH = 12
IMG_X = DERIV + SMOOTH
IMG_Y = 16
POT_X = SWEEPS
POT_Y = 8
MESH = pl.DeviceIdType.MESH
F32 = jnp.float32
BF16 = jnp.bfloat16


def gauss_taps(sigma, reach, order):
    values = [math.exp(-t * t / (2.0 * sigma * sigma)) for t in range(-reach, reach + 1)]
    total = sum(values)
    values = [value / total for value in values]
    if order == 1:
        values = [(i - reach) * values[i] / (sigma * sigma) for i in range(2 * reach + 1)]
    return values


NEAR = gauss_taps(1.0, DERIV, 0)
SLOPE = gauss_taps(1.0, DERIV, 1)
WIDE = gauss_taps(4.0, SMOOTH, 0)


def halves(matrix):
    high = matrix.astype(ml_dtypes.bfloat16)
    low = (matrix - high.astype(np.float32)).astype(ml_dtypes.bfloat16)
    return high, low


def band(out_len, in_len, margin, taps, first=0, last=None):
    reach = (len(taps) - 1) // 2
    matrix = np.zeros((out_len, in_len), np.float32)
    for i in range(first, out_len if last is None else last):
        for t in range(-reach, reach + 1):
            k = i + margin + t
            if 0 <= k < in_len:
                matrix[i, k] = taps[t + reach]
    return matrix


def left_weights(matrix):
    high, low = halves(matrix)
    return np.concatenate([high, high, low], axis=1)


def right_weights(*matrices):
    parts = []
    for matrix in matrices:
        parts += list(halves(np.ascontiguousarray(matrix.T)))
    return np.concatenate(parts, axis=1)


def neighbours():
    gx, gy = lax.axis_index("gx"), lax.axis_index("gy")
    nx, ny = lax.axis_size("gx"), lax.axis_size("gy")
    has_x = (gx > 0, gx < nx - 1)
    has_y = (gy > 0, gy < ny - 1)
    at_x = ((gx - 1, gy), (gx + 1, gy))
    at_y = ((gx, gy - 1), (gx, gy + 1))
    return has_x, has_y, at_x, at_y


def greet():
    has_x, has_y, at_x, at_y = neighbours()
    barrier = pltpu.get_barrier_semaphore()
    for has, at in zip(has_x + has_y, at_x + at_y):
        @pl.when(has)
        def _(at=at):
            pl.semaphore_signal(barrier, inc=1, device_id=at, device_id_type=MESH)
    pl.semaphore_wait(barrier, sum(has.astype(jnp.int32) for has in has_x + has_y))


class Exchange:
    def __init__(self, own, ext, hx, hy, cuts, send, recv, local):
        self.own, self.ext, self.hx, self.hy, self.cuts = own, ext, hx, hy, cuts
        self.send, self.recv, self.local = send, recv, local
        self.nx, self.ny = own.shape[0], own.shape[1]
        self.has_x, self.has_y, self.at_x, self.at_y = neighbours()

    @staticmethod
    def count(cuts):
        return 2 + 6 * len(cuts)

    def remote(self, src, dst, index, at):
        return pltpu.make_async_remote_copy(
            src_ref=src, dst_ref=dst, send_sem=self.send.at[index],
            recv_sem=self.recv.at[index], device_id=at, device_id_type=MESH)

    def halo_rows(self, d, cut):
        a, b = cut
        if d == 0:
            return self.nx + self.hx + a, b - a
        return self.hx - b, b - a

    def copy_x(self, d, c):
        a, b = self.cuts[c]
        row, size = self.halo_rows(d, (a, b))
        start = a if d == 0 else self.nx - b
        return self.remote(
            self.own.at[pl.ds(start, size)],
            self.ext.at[pl.ds(row, size), pl.ds(self.hy, self.ny)],
            2 + d * len(self.cuts) + c, self.at_x[d])

    def copy_y(self, d):
        src = 0 if d == 0 else self.ny - self.hy
        dst = self.hy + self.ny if d == 0 else 0
        return self.remote(
            self.own.at[:, pl.ds(src, self.hy)],
            self.ext.at[pl.ds(self.hx, self.nx), pl.ds(dst, self.hy)],
            d, self.at_y[d])

    def copy_corner(self, side, d, c):
        row, size = self.halo_rows(side, self.cuts[c])
        src = self.hy if d == 0 else self.ny
        dst = self.hy + self.ny if d == 0 else 0
        n = len(self.cuts)
        return self.remote(
            self.ext.at[pl.ds(row, size), pl.ds(src, self.hy)],
            self.ext.at[pl.ds(row, size), pl.ds(dst, self.hy)],
            2 + 2 * n + (side * 2 + d) * n + c, self.at_y[d])

    def copy_own(self):
        return pltpu.make_async_copy(
            self.own, self.ext.at[pl.ds(self.hx, self.nx), pl.ds(self.hy, self.ny)], self.local)

    def start(self):
        for c in range(len(self.cuts)):
            for d in range(2):
                pl.when(self.has_x[d])(lambda d=d, c=c: self.copy_x(d, c).start())
        for d in range(2):
            pl.when(self.has_y[d])(lambda d=d: self.copy_y(d).start())
        self.copy_own().start()
        rows, cols, z = self.ext.shape
        for d in range(2):
            @pl.when(jnp.logical_not(self.has_x[d]))
            def _(d=d):
                at = 0 if d == 0 else self.hx + self.nx
                self.ext[pl.ds(at, self.hx)] = jnp.zeros((self.hx, cols, z), F32)

            @pl.when(jnp.logical_not(self.has_y[d]))
            def _(d=d):
                at = 0 if d == 0 else self.hy + self.ny
                self.ext[:, pl.ds(at, self.hy)] = jnp.zeros((rows, self.hy, z), F32)

    def forward(self):
        for c in range(len(self.cuts)):
            for side in range(2):
                @pl.when(self.has_x[1 - side])
                def _(side=side, c=c):
                    self.copy_x(side, c).wait_recv()
                    for d in range(2):
                        pl.when(self.has_y[d])(
                            lambda d=d: self.copy_corner(side, d, c).start())

    def finish(self):
        self.copy_own().wait()
        for d in range(2):
            pl.when(self.has_y[1 - d])(lambda d=d: self.copy_y(d).wait_recv())
            for c in range(len(self.cuts)):
                for side in range(2):
                    pl.when(jnp.logical_and(self.has_x[1 - side], self.has_y[1 - d]))(
                        lambda d=d, c=c, side=side: self.copy_corner(side, d, c).wait_recv())
        for d in range(2):
            pl.when(self.has_y[d])(lambda d=d: self.copy_y(d).wait_send())
            for c in range(len(self.cuts)):
                pl.when(self.has_x[d])(lambda d=d, c=c: self.copy_x(d, c).wait_send())
                for side in range(2):
                    pl.when(jnp.logical_and(self.has_x[1 - side], self.has_y[d]))(
                        lambda d=d, c=c, side=side: self.copy_corner(side, d, c).wait_send())


def exchange_kernel(plans, *refs):
    n = len(plans)
    owns, exts, sems = refs[:n], refs[n:2 * n], refs[2 * n:]
    greet()
    parts = [
        Exchange(own, ext, *plan, *sems[3 * i:3 * i + 3])
        for i, (own, ext, plan) in enumerate(zip(owns, exts, plans))
    ]
    for part in parts:
        part.start()
    for part in parts:
        part.forward()
    for part in parts:
        part.finish()


def exchange(arrays, plans, collective_id):
    shapes, scratch = [], []
    for array, (hx, hy, cuts) in zip(arrays, plans):
        x, y, z = array.shape
        shapes.append(jax.ShapeDtypeStruct((x + 2 * hx, y + 2 * hy, z), F32))
        count = Exchange.count(cuts)
        scratch += [pltpu.SemaphoreType.DMA((count,))] * 2 + [pltpu.SemaphoreType.DMA]
    return pl.pallas_call(
        functools.partial(exchange_kernel, plans),
        out_shape=shapes,
        in_specs=[pl.BlockSpec(memory_space=pl.ANY)] * len(arrays),
        out_specs=[pl.BlockSpec(memory_space=pltpu.VMEM)] * len(arrays),
        scratch_shapes=scratch,
        compiler_params=pltpu.CompilerParams(
            collective_id=collective_id, has_side_effects=True,
            vmem_limit_bytes=32 * 1024 * 1024),
    )(*arrays)


def split(value):
    high = value.astype(BF16)
    return high, (value - high.astype(F32)).astype(BF16)


def dot(a, b):
    return jnp.dot(a, b, preferred_element_type=F32)


def left(weights, value):
    high, low = split(value)
    return dot(weights, jnp.concatenate([high, low, high], axis=0))


def right(value, high_w, low_w):
    high, low = split(value)
    return dot(high, high_w) + dot(low, high_w) + dot(high, low_w)


def tensor_kernel(unroll, ext, phases, table, wg, ws, zg, zs, cond, masked, along, smooth):
    gx, gy = lax.axis_index("gx"), lax.axis_index("gy")
    bx, by, z = cond.shape
    size_x, size_y = bx * lax.axis_size("gx"), by * lax.axis_size("gy")
    wide_y = ext.shape[1]
    rows_x = bx + 2 * SMOOTH

    row_y = gy * by - IMG_Y + lax.broadcasted_iota(jnp.int32, (wide_y, wg.shape[1]), 0)
    inside = jnp.logical_and(row_y >= 0, row_y < size_y)
    for k in range(2):
        part = wg[k * wide_y:(k + 1) * wide_y].astype(F32)
        masked[k * wide_y:(k + 1) * wide_y] = jnp.where(inside, part, 0.0).astype(BF16)

    def derive(step, carry):
        firsts, seconds = [], []
        for j in range(unroll):
            r = step * unroll + j
            at = gx * bx + r - SMOOTH
            ok = jnp.logical_and(at >= 0, at < size_x).astype(F32)
            e = [ext[r + t] for t in range(2 * DERIV + 1)]
            a = e[DERIV] * (NEAR[DERIV] * ok)
            b = jnp.zeros_like(a)
            for t in range(1, DERIV + 1):
                a = a + (e[DERIV + t] + e[DERIV - t]) * (NEAR[DERIV + t] * ok)
                b = b + (e[DERIV + t] - e[DERIV - t]) * (SLOPE[DERIV + t] * ok)
            y_a = left(masked[...], a)
            y_b = left(masked[:wide_y], b)
            firsts += [y_b, y_a[wide_y:]]
            seconds.append(y_a[:wide_y])
        first = right(jnp.concatenate(firsts, axis=0), zg[:, :z], zg[:, z:2 * z])
        second = right(jnp.concatenate(seconds, axis=0), zg[:, 2 * z:3 * z], zg[:, 3 * z:])
        for j in range(unroll):
            r = step * unroll + j
            g_x = first[2 * j * wide_y:(2 * j + 1) * wide_y]
            g_y = first[(2 * j + 1) * wide_y:(2 * j + 2) * wide_y]
            g_z = second[j * wide_y:(j + 1) * wide_y]
            for f, (p, q) in enumerate(
                ((g_x, g_x), (g_y, g_y), (g_z, g_z), (g_x, g_y), (g_x, g_z), (g_y, g_z))
            ):
                along[f, r] = left(ws[...], p * q)
        return carry

    lax.fori_loop(0, rows_x // unroll, derive, 0)

    tiles_y, tiles_z = by // 8, z // 128

    def smooth_x(step, carry):
        f = step // (tiles_y * tiles_z)
        ys = pl.ds(pl.multiple_of((step // tiles_z) % tiles_y * 8, 8), 8)
        zz = pl.ds(pl.multiple_of(step % tiles_z * 128, 128), 128)
        v = [along[f, r, ys, zz] for r in range(rows_x)]
        for i in range(bx):
            c = i + SMOOTH
            total = v[c] * WIDE[SMOOTH]
            for t in range(1, SMOOTH + 1):
                total = total + (v[c + t] + v[c - t]) * WIDE[SMOOTH + t]
            smooth[f, i, ys, zz] = total
        return carry

    lax.fori_loop(0, 6 * tiles_y * tiles_z, smooth_x, 0)

    def finish(i, carry):
        s = right(
            jnp.concatenate([smooth[f, i] for f in range(6)], axis=0), zs[:, :z], zs[:, z:])
        jxx, jyy, jzz, jxy, jxz, jyz = (s[f * by:(f + 1) * by] for f in range(6))
        trace = jxx + jyy + jzz
        shift = 0.1 * trace + 1e-06
        a, b, c = jxx + shift, jyy + shift, jzz + shift
        cof = a * b - jxy * jxy
        det = (
            a * (b * c - jyz * jyz)
            - jxy * (jxy * c - jyz * jxz)
            + jxz * (jxy * jyz - b * jxz)
        )
        weight = trace * cof / det
        label = phases[i]
        base = jnp.where(label == 0, table[0, 0], jnp.where(label == 1, table[0, 1], table[0, 2]))
        aniso = jnp.where(label == 0, table[1, 0], jnp.where(label == 1, table[1, 1], table[1, 2]))
        cond[i] = base + 0.1 * aniso * weight
        return carry

    lax.fori_loop(0, bx, finish, 0)


def tensor(ext, phases, table):
    bx, by, z = phases.shape
    wide_y = by + 2 * IMG_Y
    rows_x = bx + 2 * SMOOTH
    lo, hi = IMG_Y - SMOOTH, wide_y - (IMG_Y - SMOOTH)
    wg = np.concatenate([
        left_weights(band(wide_y, wide_y, 0, NEAR, lo, hi)),
        left_weights(band(wide_y, wide_y, 0, SLOPE, lo, hi)),
    ], axis=0)
    ws = left_weights(band(by, wide_y, IMG_Y, WIDE))
    zg = right_weights(band(z, z, 0, NEAR), band(z, z, 0, SLOPE))
    zs = right_weights(band(z, z, 0, WIDE))
    vmem = pl.BlockSpec(memory_space=pltpu.VMEM)
    return pl.pallas_call(
        functools.partial(tensor_kernel, 4),
        out_shape=jax.ShapeDtypeStruct((bx, by, z), F32),
        in_specs=[vmem, vmem, pl.BlockSpec(memory_space=pltpu.SMEM)] + [vmem] * 4,
        out_specs=vmem,
        scratch_shapes=[
            pltpu.VMEM(wg.shape, BF16),
            pltpu.VMEM((6, rows_x, by, z), F32),
            pltpu.VMEM((6, bx, by, z), F32),
        ],
        compiler_params=pltpu.CompilerParams(vmem_limit_bytes=48 * 1024 * 1024),
    )(ext, phases, table, wg, ws, zg, zs)


def harmonic(p, q):
    total = p + q
    return 2.0 * p * q / jnp.where(total > 0, total, 1.0)


def sweep_kernel(cond, start, out, kx, ky, k0, k1, inv, one, two):
    rows, wide, z = cond.shape
    lane = lax.broadcasted_iota(jnp.int32, (wide, z), 1)
    at_low, at_high = lane == 0, lane == z - 1

    def roll_y(v, s):
        return pltpu.roll(v, s % wide, 0)

    def roll_z(v, s):
        return pltpu.roll(v, s % z, 1)

    kx[0] = harmonic(cond[0], cond[1])

    def coefficients(j, carry):
        c = cond[j]
        upper = harmonic(c, cond[j + 1])
        kx[j] = upper
        y_up = harmonic(c, roll_y(c, -1))
        ky[j] = y_up
        z_up = harmonic(c, roll_z(c, -1))
        low = jnp.where(at_low, c, roll_z(z_up, 1))
        high = jnp.where(at_high, c, z_up)
        k0[j] = low
        k1[j] = high
        total = kx[j - 1] + upper + roll_y(y_up, 1) + y_up + low + high
        inv[j] = 1.0 / jnp.where(total > 0, total, 1.0)
        return carry

    lax.fori_loop(1, rows - 1, coefficients, 0)

    def sweep(src, dst, first, last):
        def step(j, carry):
            p = src[j]
            y_up = ky[j]
            numer = kx[j - 1] * src[j - 1] + kx[j] * src[j + 1]
            numer = numer + roll_y(y_up, 1) * roll_y(p, 1) + y_up * roll_y(p, -1)
            numer = numer + k0[j] * jnp.where(at_low, 1.0, roll_z(p, 1))
            numer = numer + k1[j] * jnp.where(at_high, 0.0, roll_z(p, -1))
            dst(j, numer * inv[j])
            return carry
        lax.fori_loop(first, last, step, 0)

    def into(ref):
        def put(j, v):
            ref[j] = v
        return put

    def put_out(j, v):
        out[j - POT_X] = v[POT_Y:wide - POT_Y]

    sweep(start, into(one), 1, rows - 1)
    sweep(one, into(two), 2, rows - 2)
    sweep(two, put_out, 3, rows - 3)


def sweeps(cond_ext, pot_ext):
    rows, wide, z = cond_ext.shape
    vmem = pl.BlockSpec(memory_space=pltpu.VMEM)
    return pl.pallas_call(
        sweep_kernel,
        out_shape=jax.ShapeDtypeStruct((rows - 2 * POT_X, wide - 2 * POT_Y, z), F32),
        in_specs=[vmem, vmem],
        out_specs=vmem,
        scratch_shapes=[pltpu.VMEM((rows, wide, z), F32)] * 7,
        compiler_params=pltpu.CompilerParams(vmem_limit_bytes=32 * 1024 * 1024),
    )(cond_ext, pot_ext)


def body(image, phases, phase_table, start_potential):
    image_cuts = ((0, 5), (5, 10), (10, 15))
    pot_cuts = ((0, 3),)
    (ext,) = exchange([image], [(IMG_X, IMG_Y, image_cuts)], 0)
    conductivity = tensor(ext, phases, phase_table)
    plan = (POT_X, POT_Y, pot_cuts)
    cond_ext, pot_ext = exchange([conductivity, start_potential], [plan, plan], 1)
    return conductivity, sweeps(cond_ext, pot_ext)


def solution(mesh):
    placed = (P("gx", "gy", None), P("gx", "gy", None), P(), P("gx", "gy", None))
    return jax.shard_map(
        body,
        mesh=mesh,
        in_specs=placed,
        out_specs=(P("gx", "gy", None), P("gx", "gy", None)),
        check_vma=False,
    )
```

```python
import functools
import math

import jax
import jax.numpy as jnp
import ml_dtypes
import numpy as np
from jax import lax
from jax.experimental import pallas as pl
from jax.experimental.pallas import tpu as pltpu
from jax.sharding import PartitionSpec as P

SWEEPS = 3
PHASES = 3
DERIV = 3
SMOOTH = 12
IMG_X = DERIV + SMOOTH
IMG_Y = 16
POT_X = SWEEPS
POT_Y = 8
MESH = pl.DeviceIdType.MESH
F32 = jnp.float32
BF16 = jnp.bfloat16


def gauss_taps(sigma, reach, order):
    values = [math.exp(-t * t / (2.0 * sigma * sigma)) for t in range(-reach, reach + 1)]
    total = sum(values)
    values = [value / total for value in values]
    if order == 1:
        values = [(i - reach) * values[i] / (sigma * sigma) for i in range(2 * reach + 1)]
    return values


NEAR = gauss_taps(1.0, DERIV, 0)
SLOPE = gauss_taps(1.0, DERIV, 1)
WIDE = gauss_taps(4.0, SMOOTH, 0)


def halves(matrix):
    high = matrix.astype(ml_dtypes.bfloat16)
    low = (matrix - high.astype(np.float32)).astype(ml_dtypes.bfloat16)
    return high, low


def band(out_len, in_len, margin, taps, first=0, last=None):
    reach = (len(taps) - 1) // 2
    matrix = np.zeros((out_len, in_len), np.float32)
    for i in range(first, out_len if last is None else last):
        for t in range(-reach, reach + 1):
            k = i + margin + t
            if 0 <= k < in_len:
                matrix[i, k] = taps[t + reach]
    return matrix


def left_weights(matrix):
    high, low = halves(matrix)
    return np.concatenate([high, high, low], axis=1)


def right_weights(*matrices):
    parts = []
    for matrix in matrices:
        parts += list(halves(np.ascontiguousarray(matrix.T)))
    return np.concatenate(parts, axis=1)


def neighbours():
    gx, gy = lax.axis_index("gx"), lax.axis_index("gy")
    nx, ny = lax.axis_size("gx"), lax.axis_size("gy")
    has_x = (gx > 0, gx < nx - 1)
    has_y = (gy > 0, gy < ny - 1)
    at_x = ((gx - 1, gy), (gx + 1, gy))
    at_y = ((gx, gy - 1), (gx, gy + 1))
    return has_x, has_y, at_x, at_y


def greet():
    has_x, has_y, at_x, at_y = neighbours()
    barrier = pltpu.get_barrier_semaphore()
    for has, at in zip(has_x + has_y, at_x + at_y):
        @pl.when(has)
        def _(at=at):
            pl.semaphore_signal(barrier, inc=1, device_id=at, device_id_type=MESH)
    pl.semaphore_wait(barrier, sum(has.astype(jnp.int32) for has in has_x + has_y))


class Exchange:
    def __init__(self, own, ext, hx, hy, cuts, bands, send, recv):
        self.ext, self.hx, self.hy, self.cuts, self.bands = ext, hx, hy, cuts, bands
        self.send, self.recv = send, recv
        self.nx, self.ny = ext.shape[0] - 2 * hx, ext.shape[1] - 2 * hy
        self.own = own
        self.has_x, self.has_y, self.at_x, self.at_y = neighbours()

    @staticmethod
    def count(cuts, bands):
        return 2 * len(bands) + 6 * len(cuts)

    def remote(self, src, dst, index, at):
        return pltpu.make_async_remote_copy(
            src_ref=src, dst_ref=dst, send_sem=self.send.at[index],
            recv_sem=self.recv.at[index], device_id=at, device_id_type=MESH)

    def brick(self, row, rows, col, cols):
        if self.own is None:
            return self.ext.at[pl.ds(self.hx + row, rows), pl.ds(self.hy + col, cols)]
        return self.own.at[pl.ds(row, rows), pl.ds(col, cols)]

    def halo_rows(self, d, cut):
        a, b = cut
        if d == 0:
            return self.nx + self.hx + a, b - a
        return self.hx - b, b - a

    def copy_x(self, d, c):
        a, b = self.cuts[c]
        row, size = self.halo_rows(d, (a, b))
        start = a if d == 0 else self.nx - b
        return self.remote(
            self.brick(start, size, 0, self.ny),
            self.ext.at[pl.ds(row, size), pl.ds(self.hy, self.ny)],
            d * len(self.cuts) + c, self.at_x[d])

    def copy_y(self, d, k):
        a, b = self.bands[k]
        src = 0 if d == 0 else self.ny - self.hy
        dst = self.hy + self.ny if d == 0 else 0
        return self.remote(
            self.brick(a, b - a, src, self.hy),
            self.ext.at[pl.ds(self.hx + a, b - a), pl.ds(dst, self.hy)],
            6 * len(self.cuts) + d * len(self.bands) + k, self.at_y[d])

    def copy_corner(self, side, d, c):
        row, size = self.halo_rows(side, self.cuts[c])
        src = self.hy if d == 0 else self.ny
        dst = self.hy + self.ny if d == 0 else 0
        n = len(self.cuts)
        return self.remote(
            self.ext.at[pl.ds(row, size), pl.ds(src, self.hy)],
            self.ext.at[pl.ds(row, size), pl.ds(dst, self.hy)],
            2 * n + (side * 2 + d) * n + c, self.at_y[d])

    def start_x(self, c):
        for d in range(2):
            pl.when(self.has_x[d])(lambda d=d: self.copy_x(d, c).start())

    def start_y(self, k):
        for d in range(2):
            pl.when(self.has_y[d])(lambda d=d: self.copy_y(d, k).start())

    def clear(self):
        rows, cols, z = self.ext.shape
        for d in range(2):
            @pl.when(jnp.logical_not(self.has_x[d]))
            def _(d=d):
                at = 0 if d == 0 else self.hx + self.nx
                self.ext[pl.ds(at, self.hx)] = jnp.zeros((self.hx, cols, z), F32)

            @pl.when(jnp.logical_not(self.has_y[d]))
            def _(d=d):
                at = 0 if d == 0 else self.hy + self.ny
                self.ext[:, pl.ds(at, self.hy)] = jnp.zeros((rows, self.hy, z), F32)

    def forward(self, c):
        for side in range(2):
            @pl.when(self.has_x[1 - side])
            def _(side=side):
                self.copy_x(side, c).wait_recv()
                for d in range(2):
                    pl.when(self.has_y[d])(lambda d=d: self.copy_corner(side, d, c).start())

    def wait_y(self, k):
        for d in range(2):
            pl.when(self.has_y[1 - d])(lambda d=d: self.copy_y(d, k).wait_recv())

    def wait_corner(self, c):
        for side in range(2):
            for d in range(2):
                pl.when(jnp.logical_and(self.has_x[1 - side], self.has_y[1 - d]))(
                    lambda d=d, side=side: self.copy_corner(side, d, c).wait_recv())

    def wait_sends(self):
        for d in range(2):
            for k in range(len(self.bands)):
                pl.when(self.has_y[d])(lambda d=d, k=k: self.copy_y(d, k).wait_send())
            for c in range(len(self.cuts)):
                pl.when(self.has_x[d])(lambda d=d, c=c: self.copy_x(d, c).wait_send())
                for side in range(2):
                    pl.when(jnp.logical_and(self.has_x[1 - side], self.has_y[d]))(
                        lambda d=d, c=c, side=side: self.copy_corner(side, d, c).wait_send())


def split(value):
    high = value.astype(BF16)
    return high, (value - high.astype(F32)).astype(BF16)


def dot(a, b):
    return jnp.dot(a, b, preferred_element_type=F32)


def left(weights, value):
    high, low = split(value)
    return dot(weights, jnp.concatenate([high, low, high], axis=0))


def right(value, high_w, low_w):
    high, low = split(value)
    return dot(high, high_w) + dot(low, high_w) + dot(high, low_w)


STEP = 5
IMG_CUTS = tuple((a, a + STEP) for a in range(0, IMG_X, STEP))
POT_CUTS = ((0, POT_X),)


def brick_bands(bx):
    middle = bx // 2
    return ((0, POT_X), (bx - POT_X, bx), (POT_X, middle), (middle, bx - POT_X))


def tensor_kernel(image, phases, table, start, wg, ws, zg, zs, cond, pot,
                  ext, masked, along, smooth, *sems):
    gx, gy = lax.axis_index("gx"), lax.axis_index("gy")
    bx, by, z = phases.shape
    size_x, size_y = bx * lax.axis_size("gx"), by * lax.axis_size("gy")
    wide_y = ext.shape[1]
    rows_x = bx + 2 * SMOOTH
    bands = brick_bands(bx)

    img = Exchange(image, ext, IMG_X, IMG_Y, IMG_CUTS, ((0, bx),), *sems[0:2])
    pots = Exchange(start, pot, POT_X, POT_Y, POT_CUTS, ((0, bx),), *sems[2:4])
    conds = Exchange(None, cond, POT_X, POT_Y, POT_CUTS, bands, *sems[4:6])
    own_image = pltpu.make_async_copy(
        image, ext.at[pl.ds(IMG_X, bx), pl.ds(IMG_Y, by)], sems[6])
    own_start = pltpu.make_async_copy(
        start, pot.at[pl.ds(POT_X, bx), pl.ds(POT_Y, by)], sems[7])

    own_image.start()
    greet()
    img.start_x(0)
    img.start_y(0)
    for c in range(1, len(IMG_CUTS)):
        img.start_x(c)
    own_start.start()
    for part in (img, pots, conds):
        part.clear()

    row_y = gy * by - IMG_Y + lax.broadcasted_iota(jnp.int32, (wide_y, wg.shape[1]), 0)
    inside = jnp.logical_and(row_y >= 0, row_y < size_y)
    for k in range(2):
        part = wg[k * wide_y:(k + 1) * wide_y].astype(F32)
        masked[k * wide_y:(k + 1) * wide_y] = jnp.where(inside, part, 0.0).astype(BF16)
    own_image.wait()

    def derive(row):
        firsts, seconds = [], []
        for j in range(STEP):
            r = row + j
            at = gx * bx + r - SMOOTH
            ok = jnp.logical_and(at >= 0, at < size_x).astype(F32)
            e = [ext[r + t] for t in range(2 * DERIV + 1)]
            a = e[DERIV] * (NEAR[DERIV] * ok)
            b = jnp.zeros_like(a)
            for t in range(1, DERIV + 1):
                a = a + (e[DERIV + t] + e[DERIV - t]) * (NEAR[DERIV + t] * ok)
                b = b + (e[DERIV + t] - e[DERIV - t]) * (SLOPE[DERIV + t] * ok)
            y_a = left(masked[...], a)
            y_b = left(masked[:wide_y], b)
            firsts += [y_b, y_a[wide_y:]]
            seconds.append(y_a[:wide_y])
        first = right(jnp.concatenate(firsts, axis=0), zg[:, :z], zg[:, z:2 * z])
        second = right(jnp.concatenate(seconds, axis=0), zg[:, 2 * z:3 * z], zg[:, 3 * z:])
        for j in range(STEP):
            r = row + j
            g_x = first[2 * j * wide_y:(2 * j + 1) * wide_y]
            g_y = first[(2 * j + 1) * wide_y:(2 * j + 2) * wide_y]
            g_z = second[j * wide_y:(j + 1) * wide_y]
            for f, (p, q) in enumerate(
                ((g_x, g_x), (g_y, g_y), (g_z, g_z), (g_x, g_y), (g_x, g_z), (g_y, g_z))
            ):
                along[f, r] = left(ws[...], p * q)

    def derive_both(low, high):
        def step(k, carry):
            derive(low + k * (high - low))
            return carry
        lax.fori_loop(0, 2, step, 0)

    centre = rows_x // 2
    img.forward(0)
    img.wait_y(0)
    img.forward(1)
    derive_both(centre - STEP, centre)
    img.forward(2)
    pots.start_x(0)
    pots.start_y(0)
    for c in range(len(IMG_CUTS)):
        img.wait_corner(c)
        derive_both(centre - (c + 2) * STEP, centre + (c + 1) * STEP)

    pots.forward(0)
    tiles_y, tiles_z = by // 8, z // 128

    def smooth_x(step, carry):
        f = step // (tiles_y * tiles_z)
        ys = pl.ds(pl.multiple_of((step // tiles_z) % tiles_y * 8, 8), 8)
        zz = pl.ds(pl.multiple_of(step % tiles_z * 128, 128), 128)
        v = [along[f, r, ys, zz] for r in range(rows_x)]
        for i in range(bx):
            c = i + SMOOTH
            total = v[c] * WIDE[SMOOTH]
            for t in range(1, SMOOTH + 1):
                total = total + (v[c + t] + v[c - t]) * WIDE[SMOOTH + t]
            smooth[f, i, ys, zz] = total
        return carry

    lax.fori_loop(0, 6 * tiles_y * tiles_z, smooth_x, 0)

    def finish(i, carry):
        s = right(
            jnp.concatenate([smooth[f, i] for f in range(6)], axis=0), zs[:, :z], zs[:, z:])
        jxx, jyy, jzz, jxy, jxz, jyz = (s[f * by:(f + 1) * by] for f in range(6))
        trace = jxx + jyy + jzz
        shift = 0.1 * trace + 1e-06
        a, b, c = jxx + shift, jyy + shift, jzz + shift
        cof = a * b - jxy * jxy
        det = (
            a * (b * c - jyz * jyz)
            - jxy * (jxy * c - jyz * jxz)
            + jxz * (jxy * jyz - b * jxz)
        )
        weight = trace * cof / det
        label = phases[i]
        base = jnp.where(label == 0, table[0, 0], jnp.where(label == 1, table[0, 1], table[0, 2]))
        aniso = jnp.where(label == 0, table[1, 0], jnp.where(label == 1, table[1, 1], table[1, 2]))
        cond[POT_X + i, POT_Y:POT_Y + by] = base + 0.1 * aniso * weight
        return carry

    for k, (low, high) in enumerate(bands):
        lax.fori_loop(low, high, finish, 0)
        if k == 1:
            conds.start_x(0)
            conds.start_y(0)
        if k >= 1:
            conds.start_y(k)
    conds.forward(0)

    own_start.wait()
    pots.wait_y(0)
    pots.wait_corner(0)
    for k in range(len(bands)):
        conds.wait_y(k)
    conds.wait_corner(0)
    for part in (img, pots, conds):
        part.wait_sends()


def tensor(image, phases, table, start):
    bx, by, z = phases.shape
    wide_y = by + 2 * IMG_Y
    rows_x = bx + 2 * SMOOTH
    lo, hi = IMG_Y - SMOOTH, wide_y - (IMG_Y - SMOOTH)
    wg = np.concatenate([
        left_weights(band(wide_y, wide_y, 0, NEAR, lo, hi)),
        left_weights(band(wide_y, wide_y, 0, SLOPE, lo, hi)),
    ], axis=0)
    ws = left_weights(band(by, wide_y, IMG_Y, WIDE))
    zg = right_weights(band(z, z, 0, NEAR), band(z, z, 0, SLOPE))
    zs = right_weights(band(z, z, 0, WIDE))
    vmem = pl.BlockSpec(memory_space=pltpu.VMEM)
    hbm = pl.BlockSpec(memory_space=pltpu.HBM)
    outer = jax.ShapeDtypeStruct((bx + 2 * POT_X, by + 2 * POT_Y, z), F32)
    sems = []
    for count in (
        Exchange.count(IMG_CUTS, ((0, bx),)),
        Exchange.count(POT_CUTS, ((0, bx),)),
        Exchange.count(POT_CUTS, brick_bands(bx)),
    ):
        sems += [pltpu.SemaphoreType.DMA((count,))] * 2
    return pl.pallas_call(
        tensor_kernel,
        out_shape=[outer, outer],
        in_specs=[hbm, vmem, pl.BlockSpec(memory_space=pltpu.SMEM), hbm] + [vmem] * 4,
        out_specs=[vmem, vmem],
        scratch_shapes=[
            pltpu.VMEM((bx + 2 * IMG_X, wide_y, z), F32),
            pltpu.VMEM(wg.shape, BF16),
            pltpu.VMEM((6, rows_x, by, z), F32),
            pltpu.VMEM((6, bx, by, z), F32),
        ] + sems + [pltpu.SemaphoreType.DMA] * 2,
        compiler_params=pltpu.CompilerParams(
            collective_id=0, has_side_effects=True, vmem_limit_bytes=44 * 1024 * 1024),
    )(image, phases, table, start, wg, ws, zg, zs)


def harmonic(p, q):
    total = p + q
    return 2.0 * p * q / jnp.where(total > 0, total, 1.0)


def sweep_kernel(cond, start, centre, out, kx, ky, k0, k1, inv, one, two, sem):
    rows, wide, z = cond.shape
    copy = pltpu.make_async_copy(
        cond.at[pl.ds(POT_X, rows - 2 * POT_X), pl.ds(POT_Y, wide - 2 * POT_Y)], centre, sem)
    copy.start()
    lane = lax.broadcasted_iota(jnp.int32, (wide, z), 1)
    at_low, at_high = lane == 0, lane == z - 1

    def roll_y(v, s):
        return pltpu.roll(v, s % wide, 0)

    def roll_z(v, s):
        return pltpu.roll(v, s % z, 1)

    kx[0] = harmonic(cond[0], cond[1])

    def coefficients(j, carry):
        c = cond[j]
        upper = harmonic(c, cond[j + 1])
        kx[j] = upper
        y_up = harmonic(c, roll_y(c, -1))
        ky[j] = y_up
        z_up = harmonic(c, roll_z(c, -1))
        low = jnp.where(at_low, c, roll_z(z_up, 1))
        high = jnp.where(at_high, c, z_up)
        k0[j] = low
        k1[j] = high
        total = kx[j - 1] + upper + roll_y(y_up, 1) + y_up + low + high
        inv[j] = 1.0 / jnp.where(total > 0, total, 1.0)
        return carry

    lax.fori_loop(1, rows - 1, coefficients, 0)

    def sweep(src, dst, first, last):
        def step(j, carry):
            p = src[j]
            y_up = ky[j]
            numer = kx[j - 1] * src[j - 1] + kx[j] * src[j + 1]
            numer = numer + roll_y(y_up, 1) * roll_y(p, 1) + y_up * roll_y(p, -1)
            numer = numer + k0[j] * jnp.where(at_low, 1.0, roll_z(p, 1))
            numer = numer + k1[j] * jnp.where(at_high, 0.0, roll_z(p, -1))
            dst(j, numer * inv[j])
            return carry
        lax.fori_loop(first, last, step, 0)

    def into(ref):
        def put(j, v):
            ref[j] = v
        return put

    def put_out(j, v):
        out[j - POT_X] = v[POT_Y:wide - POT_Y]

    sweep(start, into(one), 1, rows - 1)
    sweep(one, into(two), 2, rows - 2)
    sweep(two, put_out, 3, rows - 3)
    copy.wait()


def sweeps(cond_ext, pot_ext):
    rows, wide, z = cond_ext.shape
    vmem = pl.BlockSpec(memory_space=pltpu.VMEM)
    brick = jax.ShapeDtypeStruct((rows - 2 * POT_X, wide - 2 * POT_Y, z), F32)
    return pl.pallas_call(
        sweep_kernel,
        out_shape=[brick, brick],
        in_specs=[vmem, vmem],
        out_specs=[pl.BlockSpec(memory_space=pltpu.HBM), vmem],
        scratch_shapes=[pltpu.VMEM((rows, wide, z), F32)] * 7 + [pltpu.SemaphoreType.DMA],
        compiler_params=pltpu.CompilerParams(vmem_limit_bytes=32 * 1024 * 1024),
    )(cond_ext, pot_ext)


def body(image, phases, phase_table, start_potential):
    cond_ext, pot_ext = tensor(image, phases, phase_table, start_potential)
    conductivity, potential = sweeps(cond_ext, pot_ext)
    return conductivity, potential


def solution(mesh):
    placed = (P("gx", "gy", None), P("gx", "gy", None), P(), P("gx", "gy", None))
    return jax.shard_map(
        body,
        mesh=mesh,
        in_specs=placed,
        out_specs=(P("gx", "gy", None), P("gx", "gy", None)),
        check_vma=False,
    )
```

```python
import functools
import math

import jax
import jax.numpy as jnp
import ml_dtypes
import numpy as np
from jax import lax
from jax.experimental import pallas as pl
from jax.experimental.pallas import tpu as pltpu
from jax.sharding import PartitionSpec as P

SWEEPS = 3
PHASES = 3
DERIV = 3
SMOOTH = 12
IMG_X = DERIV + SMOOTH
IMG_Y = 16
POT_X = SWEEPS
POT_Y = 8
MESH = pl.DeviceIdType.MESH
VMEM_LIMIT = 58 * 1024 * 1024
F32 = jnp.float32
BF16 = jnp.bfloat16


def gauss_taps(sigma, reach, order):
    values = [math.exp(-t * t / (2.0 * sigma * sigma)) for t in range(-reach, reach + 1)]
    total = sum(values)
    values = [value / total for value in values]
    if order == 1:
        values = [(i - reach) * values[i] / (sigma * sigma) for i in range(2 * reach + 1)]
    return values


NEAR = gauss_taps(1.0, DERIV, 0)
SLOPE = gauss_taps(1.0, DERIV, 1)
WIDE = gauss_taps(4.0, SMOOTH, 0)


def halves(matrix):
    high = matrix.astype(ml_dtypes.bfloat16)
    low = (matrix - high.astype(np.float32)).astype(ml_dtypes.bfloat16)
    return high, low


def band(out_len, in_len, margin, taps, first=0, last=None):
    reach = (len(taps) - 1) // 2
    matrix = np.zeros((out_len, in_len), np.float32)
    for i in range(first, out_len if last is None else last):
        for t in range(-reach, reach + 1):
            k = i + margin + t
            if 0 <= k < in_len:
                matrix[i, k] = taps[t + reach]
    return matrix


def left_weights(matrix):
    high, low = halves(matrix)
    return np.concatenate([high, high, low], axis=1)


def right_weights(*matrices):
    parts = []
    for matrix in matrices:
        parts += list(halves(np.ascontiguousarray(matrix.T)))
    return np.concatenate(parts, axis=1)


def neighbours():
    gx, gy = lax.axis_index("gx"), lax.axis_index("gy")
    nx, ny = lax.axis_size("gx"), lax.axis_size("gy")
    has_x = (gx > 0, gx < nx - 1)
    has_y = (gy > 0, gy < ny - 1)
    at_x = ((gx - 1, gy), (gx + 1, gy))
    at_y = ((gx, gy - 1), (gx, gy + 1))
    return has_x, has_y, at_x, at_y


def greet():
    has_x, has_y, at_x, at_y = neighbours()
    barrier = pltpu.get_barrier_semaphore()
    for has, at in zip(has_x + has_y, at_x + at_y):
        @pl.when(has)
        def _(at=at):
            pl.semaphore_signal(barrier, inc=1, device_id=at, device_id_type=MESH)
    pl.semaphore_wait(barrier, sum(has.astype(jnp.int32) for has in has_x + has_y))


class Exchange:
    def __init__(self, own, ext, hx, hy, cuts, bands, send, recv):
        self.ext, self.hx, self.hy, self.cuts, self.bands = ext, hx, hy, cuts, bands
        self.send, self.recv = send, recv
        self.nx, self.ny = ext.shape[0] - 2 * hx, ext.shape[1] - 2 * hy
        self.own = own
        self.has_x, self.has_y, self.at_x, self.at_y = neighbours()

    @staticmethod
    def count(cuts, bands):
        return 2 * len(bands) + 6 * len(cuts)

    def remote(self, src, dst, index, at):
        return pltpu.make_async_remote_copy(
            src_ref=src, dst_ref=dst, send_sem=self.send.at[index],
            recv_sem=self.recv.at[index], device_id=at, device_id_type=MESH)

    def brick(self, row, rows, col, cols):
        if self.own is None:
            return self.ext.at[pl.ds(self.hx + row, rows), pl.ds(self.hy + col, cols)]
        return self.own.at[pl.ds(row, rows), pl.ds(col, cols)]

    def halo_rows(self, d, cut):
        a, b = cut
        if d == 0:
            return self.nx + self.hx + a, b - a
        return self.hx - b, b - a

    def copy_x(self, d, c):
        a, b = self.cuts[c]
        row, size = self.halo_rows(d, (a, b))
        start = a if d == 0 else self.nx - b
        return self.remote(
            self.brick(start, size, 0, self.ny),
            self.ext.at[pl.ds(row, size), pl.ds(self.hy, self.ny)],
            d * len(self.cuts) + c, self.at_x[d])

    def copy_y(self, d, k):
        a, b = self.bands[k]
        src = 0 if d == 0 else self.ny - self.hy
        dst = self.hy + self.ny if d == 0 else 0
        return self.remote(
            self.brick(a, b - a, src, self.hy),
            self.ext.at[pl.ds(self.hx + a, b - a), pl.ds(dst, self.hy)],
            6 * len(self.cuts) + d * len(self.bands) + k, self.at_y[d])

    def copy_corner(self, side, d, c):
        row, size = self.halo_rows(side, self.cuts[c])
        src = self.hy if d == 0 else self.ny
        dst = self.hy + self.ny if d == 0 else 0
        n = len(self.cuts)
        return self.remote(
            self.ext.at[pl.ds(row, size), pl.ds(src, self.hy)],
            self.ext.at[pl.ds(row, size), pl.ds(dst, self.hy)],
            2 * n + (side * 2 + d) * n + c, self.at_y[d])

    def start_x(self, c):
        for d in range(2):
            pl.when(self.has_x[d])(lambda d=d: self.copy_x(d, c).start())

    def start_y(self, k):
        for d in range(2):
            pl.when(self.has_y[d])(lambda d=d: self.copy_y(d, k).start())

    def clear(self):
        rows, cols, z = self.ext.shape
        for d in range(2):
            @pl.when(jnp.logical_not(self.has_x[d]))
            def _(d=d):
                at = 0 if d == 0 else self.hx + self.nx
                self.ext[pl.ds(at, self.hx)] = jnp.zeros((self.hx, cols, z), F32)

            @pl.when(jnp.logical_not(self.has_y[d]))
            def _(d=d):
                at = 0 if d == 0 else self.hy + self.ny
                self.ext[:, pl.ds(at, self.hy)] = jnp.zeros((rows, self.hy, z), F32)

    def forward(self, c):
        for side in range(2):
            @pl.when(self.has_x[1 - side])
            def _(side=side):
                self.copy_x(side, c).wait_recv()
                for d in range(2):
                    pl.when(self.has_y[d])(lambda d=d: self.copy_corner(side, d, c).start())

    def wait_y(self, k):
        for d in range(2):
            pl.when(self.has_y[1 - d])(lambda d=d: self.copy_y(d, k).wait_recv())

    def wait_corner(self, c):
        for side in range(2):
            for d in range(2):
                pl.when(jnp.logical_and(self.has_x[1 - side], self.has_y[1 - d]))(
                    lambda d=d, side=side: self.copy_corner(side, d, c).wait_recv())

    def wait_sends(self):
        for d in range(2):
            for k in range(len(self.bands)):
                pl.when(self.has_y[d])(lambda d=d, k=k: self.copy_y(d, k).wait_send())
            for c in range(len(self.cuts)):
                pl.when(self.has_x[d])(lambda d=d, c=c: self.copy_x(d, c).wait_send())
                for side in range(2):
                    pl.when(jnp.logical_and(self.has_x[1 - side], self.has_y[d]))(
                        lambda d=d, c=c, side=side: self.copy_corner(side, d, c).wait_send())


def split(value):
    high = value.astype(BF16)
    return high, (value - high.astype(F32)).astype(BF16)


def dot(a, b):
    return jnp.dot(a, b, preferred_element_type=F32)


def left(weights, value):
    high, low = split(value)
    return dot(weights, jnp.concatenate([high, low, high], axis=0))


def right(value, high_w, low_w):
    high, low = split(value)
    return dot(high, high_w) + dot(low, high_w) + dot(high, low_w)


STEP = 5
IMG_CUTS = tuple((a, a + STEP) for a in range(0, IMG_X, STEP))
POT_CUTS = ((0, POT_X),)


def brick_bands(bx):
    middle = bx // 2
    return ((0, POT_X), (bx - POT_X, bx), (POT_X, middle), (middle, bx - POT_X))


def tensor_kernel(image, phases_in, table_in, start, wg_in, ws_in, zg_in, zs_in, cond, pot,
                  ext, masked, along, smooth, phases, table, wg, ws, zg, zs, *sems):
    gx, gy = lax.axis_index("gx"), lax.axis_index("gy")
    bx, by, z = phases.shape
    size_x, size_y = bx * lax.axis_size("gx"), by * lax.axis_size("gy")
    wide_y = ext.shape[1]
    rows_x = bx + 2 * SMOOTH
    bands = brick_bands(bx)

    img = Exchange(image, ext, IMG_X, IMG_Y, IMG_CUTS, ((0, bx),), *sems[0:2])
    pots = Exchange(start, pot, POT_X, POT_Y, POT_CUTS, ((0, bx),), *sems[2:4])
    conds = Exchange(None, cond, POT_X, POT_Y, POT_CUTS, bands, *sems[4:6])
    own_image = pltpu.make_async_copy(
        image, ext.at[pl.ds(IMG_X, bx), pl.ds(IMG_Y, by)], sems[6])
    own_start = pltpu.make_async_copy(
        start, pot.at[pl.ds(POT_X, bx), pl.ds(POT_Y, by)], sems[7])

    loads = [
        pltpu.make_async_copy(src, dst, sems[8 + k])
        for k, (src, dst) in enumerate((
            (wg_in, wg), (zg_in, zg), (ws_in, ws), (phases_in, phases), (zs_in, zs),
            (table_in, table)))
    ]
    own_image.start()
    for load in loads:
        load.start()
    greet()
    img.start_x(0)
    img.start_y(0)
    for c in range(1, len(IMG_CUTS)):
        img.start_x(c)
    own_start.start()
    for part in (img, pots, conds):
        part.clear()

    for load in loads[:3]:
        load.wait()
    row_y = gy * by - IMG_Y + lax.broadcasted_iota(jnp.int32, (wide_y, wg.shape[1]), 0)
    inside = jnp.logical_and(row_y >= 0, row_y < size_y)
    for k in range(2):
        part = wg[k * wide_y:(k + 1) * wide_y].astype(F32)
        masked[k * wide_y:(k + 1) * wide_y] = jnp.where(inside, part, 0.0).astype(BF16)
    own_image.wait()

    def derive(row):
        firsts, seconds = [], []
        for j in range(STEP):
            r = row + j
            at = gx * bx + r - SMOOTH
            ok = jnp.logical_and(at >= 0, at < size_x).astype(F32)
            e = [ext[r + t] for t in range(2 * DERIV + 1)]
            a = e[DERIV] * (NEAR[DERIV] * ok)
            b = jnp.zeros_like(a)
            for t in range(1, DERIV + 1):
                a = a + (e[DERIV + t] + e[DERIV - t]) * (NEAR[DERIV + t] * ok)
                b = b + (e[DERIV + t] - e[DERIV - t]) * (SLOPE[DERIV + t] * ok)
            y_a = left(masked[...], a)
            y_b = left(masked[:wide_y], b)
            firsts += [y_b, y_a[wide_y:]]
            seconds.append(y_a[:wide_y])
        first = right(jnp.concatenate(firsts, axis=0), zg[:, :z], zg[:, z:2 * z])
        second = right(jnp.concatenate(seconds, axis=0), zg[:, 2 * z:3 * z], zg[:, 3 * z:])
        for j in range(STEP):
            r = row + j
            g_x = first[2 * j * wide_y:(2 * j + 1) * wide_y]
            g_y = first[(2 * j + 1) * wide_y:(2 * j + 2) * wide_y]
            g_z = second[j * wide_y:(j + 1) * wide_y]
            for f, (p, q) in enumerate(
                ((g_x, g_x), (g_y, g_y), (g_z, g_z), (g_x, g_y), (g_x, g_z), (g_y, g_z))
            ):
                along[f, r] = left(ws[...], p * q)

    def derive_both(low, high):
        def step(k, carry):
            derive(low + k * (high - low))
            return carry
        lax.fori_loop(0, 2, step, 0)

    centre = rows_x // 2
    img.forward(0)
    img.wait_y(0)
    img.forward(1)
    derive_both(centre - STEP, centre)
    img.forward(2)
    pots.start_x(0)
    pots.start_y(0)
    for c in range(len(IMG_CUTS)):
        img.wait_corner(c)
        derive_both(centre - (c + 2) * STEP, centre + (c + 1) * STEP)

    pots.forward(0)
    for load in loads[3:]:
        load.wait()
    tiles_y, tiles_z = by // 8, z // 128

    def smooth_x(step, carry):
        f = step // (tiles_y * tiles_z)
        ys = pl.ds(pl.multiple_of((step // tiles_z) % tiles_y * 8, 8), 8)
        zz = pl.ds(pl.multiple_of(step % tiles_z * 128, 128), 128)
        v = [along[f, r, ys, zz] for r in range(rows_x)]
        for i in range(bx):
            c = i + SMOOTH
            total = v[c] * WIDE[SMOOTH]
            for t in range(1, SMOOTH + 1):
                total = total + (v[c + t] + v[c - t]) * WIDE[SMOOTH + t]
            smooth[f, i, ys, zz] = total
        return carry

    lax.fori_loop(0, 6 * tiles_y * tiles_z, smooth_x, 0)

    def finish(i, carry):
        s = right(
            jnp.concatenate([smooth[f, i] for f in range(6)], axis=0), zs[:, :z], zs[:, z:])
        jxx, jyy, jzz, jxy, jxz, jyz = (s[f * by:(f + 1) * by] for f in range(6))
        trace = jxx + jyy + jzz
        shift = 0.1 * trace + 1e-06
        a, b, c = jxx + shift, jyy + shift, jzz + shift
        cof = a * b - jxy * jxy
        det = (
            a * (b * c - jyz * jyz)
            - jxy * (jxy * c - jyz * jxz)
            + jxz * (jxy * jyz - b * jxz)
        )
        weight = trace * cof / det
        label = phases[i]
        base = jnp.where(label == 0, table[0, 0], jnp.where(label == 1, table[0, 1], table[0, 2]))
        aniso = jnp.where(label == 0, table[1, 0], jnp.where(label == 1, table[1, 1], table[1, 2]))
        cond[POT_X + i, POT_Y:POT_Y + by] = base + 0.1 * aniso * weight
        return carry

    for k, (low, high) in enumerate(bands):
        lax.fori_loop(low, high, finish, 0)
        if k == 1:
            conds.start_x(0)
            conds.start_y(0)
        if k >= 1:
            conds.start_y(k)
    conds.forward(0)

    own_start.wait()
    pots.wait_y(0)
    pots.wait_corner(0)
    for k in range(len(bands)):
        conds.wait_y(k)
    conds.wait_corner(0)
    for part in (img, pots, conds):
        part.wait_sends()


def tensor(image, phases, table, start):
    bx, by, z = phases.shape
    wide_y = by + 2 * IMG_Y
    rows_x = bx + 2 * SMOOTH
    lo, hi = IMG_Y - SMOOTH, wide_y - (IMG_Y - SMOOTH)
    wg = np.concatenate([
        left_weights(band(wide_y, wide_y, 0, NEAR, lo, hi)),
        left_weights(band(wide_y, wide_y, 0, SLOPE, lo, hi)),
    ], axis=0)
    ws = left_weights(band(by, wide_y, IMG_Y, WIDE))
    zg = right_weights(band(z, z, 0, NEAR), band(z, z, 0, SLOPE))
    zs = right_weights(band(z, z, 0, WIDE))
    vmem = pl.BlockSpec(memory_space=pltpu.VMEM)
    anywhere = pl.BlockSpec(memory_space=pl.ANY)
    outer = jax.ShapeDtypeStruct((bx + 2 * POT_X, by + 2 * POT_Y, z), F32)
    sems = []
    for count in (
        Exchange.count(IMG_CUTS, ((0, bx),)),
        Exchange.count(POT_CUTS, ((0, bx),)),
        Exchange.count(POT_CUTS, brick_bands(bx)),
    ):
        sems += [pltpu.SemaphoreType.DMA((count,))] * 2
    return pl.pallas_call(
        tensor_kernel,
        out_shape=[outer, outer],
        in_specs=[anywhere] * 8,
        out_specs=[vmem, vmem],
        scratch_shapes=[
            pltpu.VMEM((bx + 2 * IMG_X, wide_y, z), F32),
            pltpu.VMEM(wg.shape, BF16),
            pltpu.VMEM((6, rows_x, by, z), F32),
            pltpu.VMEM((6, bx, by, z), F32),
            pltpu.VMEM(phases.shape, jnp.int32),
            pltpu.SMEM(table.shape, F32),
        ] + [pltpu.VMEM(w.shape, BF16) for w in (wg, ws, zg, zs)]
        + sems + [pltpu.SemaphoreType.DMA] * 8,
        compiler_params=pltpu.CompilerParams(
            collective_id=0, has_side_effects=True, vmem_limit_bytes=VMEM_LIMIT),
    )(image, phases, table, start, wg, ws, zg, zs)


def harmonic(p, q):
    total = p + q
    return 2.0 * p * q / jnp.where(total > 0, total, 1.0)


PAIR = 2


def sweep_kernel(cond, start, centre, out, kx, y0, y1, z0, z1, inv, one, two, sem):
    rows, wide, z = cond.shape
    copy = pltpu.make_async_copy(
        cond.at[pl.ds(POT_X, rows - 2 * POT_X), pl.ds(POT_Y, wide - 2 * POT_Y)], centre, sem)
    copy.start()
    lane = lax.broadcasted_iota(jnp.int32, (PAIR, wide, z), 2)
    at_low, at_high = lane == 0, lane == z - 1

    def roll_y(v, s):
        return pltpu.roll(v, s % wide, 1)

    def roll_z(v, s):
        return pltpu.roll(v, s % z, 2)

    kx[0] = harmonic(cond[0], cond[1])

    def coefficients(step, carry):
        j = 1 + step * PAIR
        c = cond[pl.ds(j, PAIR)]
        x_up = harmonic(c, cond[pl.ds(j + 1, PAIR)])
        y_up = harmonic(c, roll_y(c, -1))
        z_up = harmonic(c, roll_z(c, -1))
        x_down = jnp.concatenate([kx[j - 1][None], x_up[:PAIR - 1]], axis=0)
        y_down = roll_y(y_up, 1)
        low = jnp.where(at_low, c, roll_z(z_up, 1))
        high = jnp.where(at_high, c, z_up)
        total = x_down + x_up + y_down + y_up + low + high
        kx[pl.ds(j, PAIR)] = x_up
        y0[pl.ds(j, PAIR)] = y_down
        y1[pl.ds(j, PAIR)] = y_up
        z0[pl.ds(j, PAIR)] = low
        z1[pl.ds(j, PAIR)] = high
        inv[pl.ds(j, PAIR)] = 1.0 / jnp.where(total > 0, total, 1.0)
        return carry

    lax.fori_loop(0, (rows - 2) // PAIR, coefficients, 0)

    def sweep(src, put, first, last):
        def step(k, carry):
            j = first + k * PAIR
            at = pl.ds(j, PAIR)
            p = src[at]
            numer = kx[pl.ds(j - 1, PAIR)] * src[pl.ds(j - 1, PAIR)]
            numer = numer + kx[at] * src[pl.ds(j + 1, PAIR)]
            numer = numer + y0[at] * roll_y(p, 1) + y1[at] * roll_y(p, -1)
            numer = numer + z0[at] * jnp.where(at_low, 1.0, roll_z(p, 1))
            numer = numer + z1[at] * jnp.where(at_high, 0.0, roll_z(p, -1))
            put(j, numer * inv[at])
            return carry
        lax.fori_loop(0, (last - first) // PAIR, step, 0)

    def into(ref):
        def put(j, v):
            ref[pl.ds(j, PAIR)] = v
        return put

    def put_out(j, v):
        out[pl.ds(j - POT_X, PAIR)] = v[:, POT_Y:wide - POT_Y]

    sweep(start, into(one), 1, rows - 1)
    sweep(one, into(two), 2, rows - 2)
    sweep(two, put_out, 3, rows - 3)
    copy.wait()


def sweeps(cond_ext, pot_ext):
    rows, wide, z = cond_ext.shape
    vmem = pl.BlockSpec(memory_space=pltpu.VMEM)
    brick = jax.ShapeDtypeStruct((rows - 2 * POT_X, wide - 2 * POT_Y, z), F32)
    return pl.pallas_call(
        sweep_kernel,
        out_shape=[brick, brick],
        in_specs=[vmem, vmem],
        out_specs=[pl.BlockSpec(memory_space=pltpu.HBM), vmem],
        scratch_shapes=[pltpu.VMEM((rows, wide, z), F32)] * 8 + [pltpu.SemaphoreType.DMA],
        compiler_params=pltpu.CompilerParams(vmem_limit_bytes=32 * 1024 * 1024),
    )(cond_ext, pot_ext)


def body(image, phases, phase_table, start_potential):
    cond_ext, pot_ext = tensor(image, phases, phase_table, start_potential)
    conductivity, potential = sweeps(cond_ext, pot_ext)
    return conductivity, potential


def solution(mesh):
    placed = (P("gx", "gy", None), P("gx", "gy", None), P(), P("gx", "gy", None))
    return jax.shard_map(
        body,
        mesh=mesh,
        in_specs=placed,
        out_specs=(P("gx", "gy", None), P("gx", "gy", None)),
        check_vma=False,
    )
```

```python
import functools
import math

import jax
import jax.numpy as jnp
import ml_dtypes
import numpy as np
from jax import lax
from jax.experimental import pallas as pl
from jax.experimental.pallas import tpu as pltpu
from jax.sharding import PartitionSpec as P

SWEEPS = 3
PHASES = 3
DERIV = 3
SMOOTH = 12
IMG_X = DERIV + SMOOTH
IMG_Y = 16
POT_X = SWEEPS
POT_Y = 8
MESH = pl.DeviceIdType.MESH
VMEM_LIMIT = 58 * 1024 * 1024
F32 = jnp.float32
BF16 = jnp.bfloat16


def gauss_taps(sigma, reach, order):
    values = [math.exp(-t * t / (2.0 * sigma * sigma)) for t in range(-reach, reach + 1)]
    total = sum(values)
    values = [value / total for value in values]
    if order == 1:
        values = [(i - reach) * values[i] / (sigma * sigma) for i in range(2 * reach + 1)]
    return values


NEAR = gauss_taps(1.0, DERIV, 0)
SLOPE = gauss_taps(1.0, DERIV, 1)
WIDE = gauss_taps(4.0, SMOOTH, 0)


def halves(matrix):
    high = matrix.astype(ml_dtypes.bfloat16)
    low = (matrix - high.astype(np.float32)).astype(ml_dtypes.bfloat16)
    return high, low


def band(out_len, in_len, margin, taps, first=0, last=None):
    reach = (len(taps) - 1) // 2
    matrix = np.zeros((out_len, in_len), np.float32)
    for i in range(first, out_len if last is None else last):
        for t in range(-reach, reach + 1):
            k = i + margin + t
            if 0 <= k < in_len:
                matrix[i, k] = taps[t + reach]
    return matrix


def left_weights(matrix):
    high, low = halves(matrix)
    return np.concatenate([high, high, low], axis=1)


def right_weights(*matrices):
    parts = []
    for matrix in matrices:
        parts += list(halves(np.ascontiguousarray(matrix.T)))
    return np.concatenate(parts, axis=1)


def neighbours():
    gx, gy = lax.axis_index("gx"), lax.axis_index("gy")
    nx, ny = lax.axis_size("gx"), lax.axis_size("gy")
    has_x = (gx > 0, gx < nx - 1)
    has_y = (gy > 0, gy < ny - 1)
    at_x = ((gx - 1, gy), (gx + 1, gy))
    at_y = ((gx, gy - 1), (gx, gy + 1))
    return has_x, has_y, at_x, at_y


def greet():
    has_x, has_y, at_x, at_y = neighbours()
    barrier = pltpu.get_barrier_semaphore()
    for has, at in zip(has_x + has_y, at_x + at_y):
        @pl.when(has)
        def _(at=at):
            pl.semaphore_signal(barrier, inc=1, device_id=at, device_id_type=MESH)
    pl.semaphore_wait(barrier, sum(has.astype(jnp.int32) for has in has_x + has_y))


class Exchange:
    def __init__(self, own, ext, hx, hy, cuts, bands, send, recv):
        self.ext, self.hx, self.hy, self.cuts, self.bands = ext, hx, hy, cuts, bands
        self.send, self.recv = send, recv
        self.nx, self.ny = ext.shape[0] - 2 * hx, ext.shape[1] - 2 * hy
        self.own = own
        self.has_x, self.has_y, self.at_x, self.at_y = neighbours()

    @staticmethod
    def count(cuts, bands):
        return 2 * len(bands) + 6 * len(cuts)

    def remote(self, src, dst, index, at):
        return pltpu.make_async_remote_copy(
            src_ref=src, dst_ref=dst, send_sem=self.send.at[index],
            recv_sem=self.recv.at[index], device_id=at, device_id_type=MESH)

    def brick(self, row, rows, col, cols):
        if self.own is None:
            return self.ext.at[pl.ds(self.hx + row, rows), pl.ds(self.hy + col, cols)]
        return self.own.at[pl.ds(row, rows), pl.ds(col, cols)]

    def halo_rows(self, d, cut):
        a, b = cut
        if d == 0:
            return self.nx + self.hx + a, b - a
        return self.hx - b, b - a

    def copy_x(self, d, c):
        a, b = self.cuts[c]
        row, size = self.halo_rows(d, (a, b))
        start = a if d == 0 else self.nx - b
        return self.remote(
            self.brick(start, size, 0, self.ny),
            self.ext.at[pl.ds(row, size), pl.ds(self.hy, self.ny)],
            d * len(self.cuts) + c, self.at_x[d])

    def copy_y(self, d, k):
        a, b = self.bands[k]
        src = 0 if d == 0 else self.ny - self.hy
        dst = self.hy + self.ny if d == 0 else 0
        return self.remote(
            self.brick(a, b - a, src, self.hy),
            self.ext.at[pl.ds(self.hx + a, b - a), pl.ds(dst, self.hy)],
            6 * len(self.cuts) + d * len(self.bands) + k, self.at_y[d])

    def copy_corner(self, side, d, c):
        row, size = self.halo_rows(side, self.cuts[c])
        src = self.hy if d == 0 else self.ny
        dst = self.hy + self.ny if d == 0 else 0
        n = len(self.cuts)
        return self.remote(
            self.ext.at[pl.ds(row, size), pl.ds(src, self.hy)],
            self.ext.at[pl.ds(row, size), pl.ds(dst, self.hy)],
            2 * n + (side * 2 + d) * n + c, self.at_y[d])

    def start_x(self, c):
        for d in range(2):
            pl.when(self.has_x[d])(lambda d=d: self.copy_x(d, c).start())

    def start_y(self, k):
        for d in range(2):
            pl.when(self.has_y[d])(lambda d=d: self.copy_y(d, k).start())

    def clear(self):
        rows, cols, z = self.ext.shape
        for d in range(2):
            @pl.when(jnp.logical_not(self.has_x[d]))
            def _(d=d):
                at = 0 if d == 0 else self.hx + self.nx
                self.ext[pl.ds(at, self.hx)] = jnp.zeros((self.hx, cols, z), F32)

            @pl.when(jnp.logical_not(self.has_y[d]))
            def _(d=d):
                at = 0 if d == 0 else self.hy + self.ny
                self.ext[:, pl.ds(at, self.hy)] = jnp.zeros((rows, self.hy, z), F32)

    def forward(self, c):
        for side in range(2):
            @pl.when(self.has_x[1 - side])
            def _(side=side):
                self.copy_x(side, c).wait_recv()
                for d in range(2):
                    pl.when(self.has_y[d])(lambda d=d: self.copy_corner(side, d, c).start())

    def wait_y(self, k):
        for d in range(2):
            pl.when(self.has_y[1 - d])(lambda d=d: self.copy_y(d, k).wait_recv())

    def wait_corner(self, c):
        for side in range(2):
            for d in range(2):
                pl.when(jnp.logical_and(self.has_x[1 - side], self.has_y[1 - d]))(
                    lambda d=d, side=side: self.copy_corner(side, d, c).wait_recv())

    def wait_sends(self):
        for d in range(2):
            for k in range(len(self.bands)):
                pl.when(self.has_y[d])(lambda d=d, k=k: self.copy_y(d, k).wait_send())
            for c in range(len(self.cuts)):
                pl.when(self.has_x[d])(lambda d=d, c=c: self.copy_x(d, c).wait_send())
                for side in range(2):
                    pl.when(jnp.logical_and(self.has_x[1 - side], self.has_y[d]))(
                        lambda d=d, c=c, side=side: self.copy_corner(side, d, c).wait_send())


def split(value):
    high = value.astype(BF16)
    return high, (value - high.astype(F32)).astype(BF16)


def dot(a, b):
    return jnp.dot(a, b, preferred_element_type=F32)


def left(weights, value):
    high, low = split(value)
    return dot(weights, jnp.concatenate([high, low, high], axis=0))


def right(value, high_w, low_w):
    high, low = split(value)
    return dot(high, high_w) + dot(low, high_w) + dot(high, low_w)


STEP = 5
IMG_CUTS = tuple((a, a + STEP) for a in range(0, IMG_X, STEP))
POT_CUTS = ((0, POT_X),)


def brick_bands(bx):
    middle = bx // 2
    return ((0, POT_X), (bx - POT_X, bx), (POT_X, middle), (middle, bx - POT_X))


def tensor_kernel(image, phases_in, table_in, start, wg_in, ws_in, zg_in, zs_in, cond, pot,
                  ext, masked, along, smooth, phases, table, wg, ws, zg, zs, *sems):
    gx, gy = lax.axis_index("gx"), lax.axis_index("gy")
    bx, by, z = phases.shape
    size_x, size_y = bx * lax.axis_size("gx"), by * lax.axis_size("gy")
    wide_y = ext.shape[1]
    rows_x = bx + 2 * SMOOTH
    bands = brick_bands(bx)

    img = Exchange(image, ext, IMG_X, IMG_Y, IMG_CUTS, ((0, bx),), *sems[0:2])
    pots = Exchange(start, pot, POT_X, POT_Y, POT_CUTS, ((0, bx),), *sems[2:4])
    conds = Exchange(None, cond, POT_X, POT_Y, POT_CUTS, bands, *sems[4:6])
    own_image = pltpu.make_async_copy(
        image, ext.at[pl.ds(IMG_X, bx), pl.ds(IMG_Y, by)], sems[6])
    own_start = pltpu.make_async_copy(
        start, pot.at[pl.ds(POT_X, bx), pl.ds(POT_Y, by)], sems[7])

    loads = [
        pltpu.make_async_copy(src, dst, sems[8 + k])
        for k, (src, dst) in enumerate((
            (wg_in, wg), (zg_in, zg), (ws_in, ws), (phases_in, phases), (zs_in, zs),
            (table_in, table)))
    ]
    own_image.start()
    for load in loads:
        load.start()
    greet()
    img.start_x(0)
    img.start_y(0)
    for c in range(1, len(IMG_CUTS)):
        img.start_x(c)
    own_start.start()
    for part in (img, pots, conds):
        part.clear()

    for load in loads[:3]:
        load.wait()
    row_y = gy * by - IMG_Y + lax.broadcasted_iota(jnp.int32, (wide_y, wg.shape[1]), 0)
    inside = jnp.logical_and(row_y >= 0, row_y < size_y)
    for k in range(2):
        part = wg[k * wide_y:(k + 1) * wide_y].astype(F32)
        masked[k * wide_y:(k + 1) * wide_y] = jnp.where(inside, part, 0.0).astype(BF16)
    own_image.wait()

    def derive(row):
        firsts, seconds = [], []
        for j in range(STEP):
            r = row + j
            at = gx * bx + r - SMOOTH
            ok = jnp.logical_and(at >= 0, at < size_x).astype(F32)
            e = [ext[r + t] for t in range(2 * DERIV + 1)]
            a = e[DERIV] * (NEAR[DERIV] * ok)
            b = jnp.zeros_like(a)
            for t in range(1, DERIV + 1):
                a = a + (e[DERIV + t] + e[DERIV - t]) * (NEAR[DERIV + t] * ok)
                b = b + (e[DERIV + t] - e[DERIV - t]) * (SLOPE[DERIV + t] * ok)
            y_a = left(masked[...], a)
            y_b = left(masked[:wide_y], b)
            firsts += [y_b, y_a[wide_y:]]
            seconds.append(y_a[:wide_y])
        first = right(jnp.concatenate(firsts, axis=0), zg[:, :z], zg[:, z:2 * z])
        second = right(jnp.concatenate(seconds, axis=0), zg[:, 2 * z:3 * z], zg[:, 3 * z:])
        for j in range(STEP):
            r = row + j
            g_x = first[2 * j * wide_y:(2 * j + 1) * wide_y]
            g_y = first[(2 * j + 1) * wide_y:(2 * j + 2) * wide_y]
            g_z = second[j * wide_y:(j + 1) * wide_y]
            for f, (p, q) in enumerate(
                ((g_x, g_x), (g_y, g_y), (g_z, g_z), (g_x, g_y), (g_x, g_z), (g_y, g_z))
            ):
                along[f, r] = left(ws[...], p * q)

    def derive_both(low, high):
        def step(k, carry):
            derive(low + k * (high - low))
            return carry
        lax.fori_loop(0, 2, step, 0)

    centre = rows_x // 2
    img.forward(0)
    img.wait_y(0)
    img.forward(1)
    derive_both(centre - STEP, centre)
    img.forward(2)
    pots.start_x(0)
    pots.start_y(0)
    tiles_y, tiles_z = by // 8, z // 128

    def smooth_x(known, ready, add):
        def step(n, carry):
            f = n // (tiles_y * tiles_z)
            ys = pl.ds(pl.multiple_of((n // tiles_z) % tiles_y * 8, 8), 8)
            zz = pl.ds(pl.multiple_of(n % tiles_z * 128, 128), 128)
            new = [r in known and r not in ready for r in range(rows_x)]
            v = [along[f, r, ys, zz] if new[r] else None for r in range(rows_x)]
            for i in range(bx):
                c = i + SMOOTH
                terms = [v[c] * WIDE[SMOOTH]] if new[c] else []
                for t in range(1, SMOOTH + 1):
                    pair = [v[r] for r in (c + t, c - t) if new[r]]
                    if pair:
                        terms.append((pair[0] + pair[1] if len(pair) > 1 else pair[0])
                                     * WIDE[SMOOTH + t])
                if terms:
                    total = smooth[f, i, ys, zz] if add else terms.pop(0)
                    for term in terms:
                        total = total + term
                    smooth[f, i, ys, zz] = total
            return carry
        lax.fori_loop(0, 6 * tiles_y * tiles_z, step, 0)

    last = len(IMG_CUTS) - 1
    for c in range(last):
        img.wait_corner(c)
        derive_both(centre - (c + 2) * STEP, centre + (c + 1) * STEP)
    inner = range(STEP, rows_x - STEP)
    smooth_x(inner, (), False)
    img.wait_corner(last)
    derive_both(0, rows_x - STEP)
    pots.forward(0)
    smooth_x(range(rows_x), inner, True)
    for load in loads[3:]:
        load.wait()

    def finish(rows):
        every = right(
            jnp.concatenate([smooth[f, i] for i in rows for f in range(6)], axis=0),
            zs[:, :z], zs[:, z:])
        for n, i in enumerate(rows):
            s = every[n * 6 * by:(n + 1) * 6 * by]
            jxx, jyy, jzz, jxy, jxz, jyz = (s[f * by:(f + 1) * by] for f in range(6))
            trace = jxx + jyy + jzz
            shift = 0.1 * trace + 1e-06
            a, b, c = jxx + shift, jyy + shift, jzz + shift
            cof = a * b - jxy * jxy
            det = (
                a * (b * c - jyz * jyz)
                - jxy * (jxy * c - jyz * jxz)
                + jxz * (jxy * jyz - b * jxz)
            )
            weight = trace * cof / det
            label = phases[i]
            base = jnp.where(
                label == 0, table[0, 0], jnp.where(label == 1, table[0, 1], table[0, 2]))
            aniso = jnp.where(
                label == 0, table[1, 0], jnp.where(label == 1, table[1, 1], table[1, 2]))
            cond[POT_X + i, POT_Y:POT_Y + by] = base + 0.1 * aniso * weight

    finish([i for low, high in bands[:2] for i in range(low, high)])
    conds.start_x(0)
    conds.start_y(0)
    conds.start_y(1)
    for k in range(2, len(bands)):
        finish(list(range(*bands[k])))
        conds.start_y(k)
    conds.forward(0)

    own_start.wait()
    pots.wait_y(0)
    pots.wait_corner(0)
    for k in range(len(bands)):
        conds.wait_y(k)
    conds.wait_corner(0)
    for part in (img, pots, conds):
        part.wait_sends()


def tensor(image, phases, table, start):
    bx, by, z = phases.shape
    wide_y = by + 2 * IMG_Y
    rows_x = bx + 2 * SMOOTH
    lo, hi = IMG_Y - SMOOTH, wide_y - (IMG_Y - SMOOTH)
    wg = np.concatenate([
        left_weights(band(wide_y, wide_y, 0, NEAR, lo, hi)),
        left_weights(band(wide_y, wide_y, 0, SLOPE, lo, hi)),
    ], axis=0)
    ws = left_weights(band(by, wide_y, IMG_Y, WIDE))
    zg = right_weights(band(z, z, 0, NEAR), band(z, z, 0, SLOPE))
    zs = right_weights(band(z, z, 0, WIDE))
    vmem = pl.BlockSpec(memory_space=pltpu.VMEM)
    anywhere = pl.BlockSpec(memory_space=pl.ANY)
    outer = jax.ShapeDtypeStruct((bx + 2 * POT_X, by + 2 * POT_Y, z), F32)
    sems = []
    for count in (
        Exchange.count(IMG_CUTS, ((0, bx),)),
        Exchange.count(POT_CUTS, ((0, bx),)),
        Exchange.count(POT_CUTS, brick_bands(bx)),
    ):
        sems += [pltpu.SemaphoreType.DMA((count,))] * 2
    return pl.pallas_call(
        tensor_kernel,
        out_shape=[outer, outer],
        in_specs=[anywhere] * 8,
        out_specs=[vmem, vmem],
        scratch_shapes=[
            pltpu.VMEM((bx + 2 * IMG_X, wide_y, z), F32),
            pltpu.VMEM(wg.shape, BF16),
            pltpu.VMEM((6, rows_x, by, z), F32),
            pltpu.VMEM((6, bx, by, z), F32),
            pltpu.VMEM(phases.shape, jnp.int32),
            pltpu.SMEM(table.shape, F32),
        ] + [pltpu.VMEM(w.shape, BF16) for w in (wg, ws, zg, zs)]
        + sems + [pltpu.SemaphoreType.DMA] * 8,
        compiler_params=pltpu.CompilerParams(
            collective_id=0, has_side_effects=True, vmem_limit_bytes=VMEM_LIMIT),
    )(image, phases, table, start, wg, ws, zg, zs)


def harmonic(p, q):
    total = p + q
    return 2.0 * p * q / jnp.where(total > 0, total, 1.0)


def step_of(count):
    return max(n for n in (1, 2, 3, 4) if count % n == 0)


def sweep_kernel(cond_in, start_in, centre, out, cond, start, kx, y0, y1, z0, z1, inv, one, two,
                 *sems):
    rows, wide, z = cond.shape
    get_cond = pltpu.make_async_copy(cond_in, cond, sems[0])
    get_start = pltpu.make_async_copy(start_in, start, sems[1])
    get_cond.start()
    get_start.start()
    get_cond.wait()
    copy = pltpu.make_async_copy(
        cond.at[pl.ds(POT_X, rows - 2 * POT_X), pl.ds(POT_Y, wide - 2 * POT_Y)], centre, sems[2])
    copy.start()
    lane = lax.broadcasted_iota(jnp.int32, (1, wide, z), 2)
    at_low, at_high = lane == 0, lane == z - 1

    def roll_y(v, s):
        return pltpu.roll(v, s % wide, 1)

    def roll_z(v, s):
        return pltpu.roll(v, s % z, 2)

    kx[0] = harmonic(cond[0], cond[1])
    size = 2

    def coefficients(step, carry):
        j = 1 + step * size
        c = cond[pl.ds(j, size)]
        x_up = harmonic(c, cond[pl.ds(j + 1, size)])
        y_up = harmonic(c, roll_y(c, -1))
        z_up = harmonic(c, roll_z(c, -1))
        x_down = jnp.concatenate([kx[j - 1][None], x_up[:size - 1]], axis=0)
        y_down = roll_y(y_up, 1)
        low = jnp.where(at_low, c, roll_z(z_up, 1))
        high = jnp.where(at_high, c, z_up)
        total = x_down + x_up + y_down + y_up + low + high
        kx[pl.ds(j, size)] = x_up
        y0[pl.ds(j, size)] = y_down
        y1[pl.ds(j, size)] = y_up
        z0[pl.ds(j, size)] = low
        z1[pl.ds(j, size)] = high
        inv[pl.ds(j, size)] = 1.0 / jnp.where(total > 0, total, 1.0)
        return carry

    lax.fori_loop(0, (rows - 2) // size, coefficients, 0)
    get_start.wait()

    def sweep(src, dst, shift, cols, first, last):
        size = step_of(last - first)

        def step(k, carry):
            j = first + k * size
            at = pl.ds(j, size)
            p = src[at]
            numer = kx[pl.ds(j - 1, size)] * src[pl.ds(j - 1, size)]
            numer = numer + kx[at] * src[pl.ds(j + 1, size)]
            numer = numer + y0[at] * roll_y(p, 1) + y1[at] * roll_y(p, -1)
            numer = numer + z0[at] * jnp.where(at_low, 1.0, roll_z(p, 1))
            numer = numer + z1[at] * jnp.where(at_high, 0.0, roll_z(p, -1))
            value = numer * inv[at]
            dst[pl.ds(j - shift, size)] = value[:, cols:wide - cols]
            return carry
        lax.fori_loop(0, (last - first) // size, step, 0)

    sweep(start, one, 0, 0, 1, rows - 1)
    sweep(one, two, 0, 0, 2, rows - 2)
    sweep(two, out, POT_X, POT_Y, 3, rows - 3)
    copy.wait()


def sweeps(cond_ext, pot_ext):
    rows, wide, z = cond_ext.shape
    vmem = pl.BlockSpec(memory_space=pltpu.VMEM)
    brick = jax.ShapeDtypeStruct((rows - 2 * POT_X, wide - 2 * POT_Y, z), F32)
    return pl.pallas_call(
        sweep_kernel,
        out_shape=[brick, brick],
        in_specs=[pl.BlockSpec(memory_space=pl.ANY)] * 2,
        out_specs=[pl.BlockSpec(memory_space=pl.ANY), vmem],
        scratch_shapes=[pltpu.VMEM((rows, wide, z), F32)] * 10 + [pltpu.SemaphoreType.DMA] * 3,
        compiler_params=pltpu.CompilerParams(vmem_limit_bytes=VMEM_LIMIT),
    )(cond_ext, pot_ext)


def body(image, phases, phase_table, start_potential):
    cond_ext, pot_ext = tensor(image, phases, phase_table, start_potential)
    conductivity, potential = sweeps(cond_ext, pot_ext)
    return conductivity, potential


def solution(mesh):
    placed = (P("gx", "gy", None), P("gx", "gy", None), P(), P("gx", "gy", None))
    return jax.shard_map(
        body,
        mesh=mesh,
        in_specs=placed,
        out_specs=(P("gx", "gy", None), P("gx", "gy", None)),
        check_vma=False,
    )
```

```python
import functools
import math

import jax
import jax.numpy as jnp
import ml_dtypes
import numpy as np
from jax import lax
from jax.experimental import pallas as pl
from jax.experimental.pallas import tpu as pltpu
from jax.sharding import PartitionSpec as P

SWEEPS = 3
PHASES = 3
DERIV = 3
SMOOTH = 12
IMG_X = DERIV + SMOOTH
IMG_Y = 16
POT_X = SWEEPS
POT_Y = 8
MESH = pl.DeviceIdType.MESH
VMEM_LIMIT = 58 * 1024 * 1024
F32 = jnp.float32
BF16 = jnp.bfloat16


def gauss_taps(sigma, reach, order):
    values = [math.exp(-t * t / (2.0 * sigma * sigma)) for t in range(-reach, reach + 1)]
    total = sum(values)
    values = [value / total for value in values]
    if order == 1:
        values = [(i - reach) * values[i] / (sigma * sigma) for i in range(2 * reach + 1)]
    return values


NEAR = gauss_taps(1.0, DERIV, 0)
SLOPE = gauss_taps(1.0, DERIV, 1)
WIDE = gauss_taps(4.0, SMOOTH, 0)


def halves(matrix):
    high = matrix.astype(ml_dtypes.bfloat16)
    low = (matrix - high.astype(np.float32)).astype(ml_dtypes.bfloat16)
    return high, low


def band(out_len, in_len, margin, taps, first=0, last=None):
    reach = (len(taps) - 1) // 2
    matrix = np.zeros((out_len, in_len), np.float32)
    for i in range(first, out_len if last is None else last):
        for t in range(-reach, reach + 1):
            k = i + margin + t
            if 0 <= k < in_len:
                matrix[i, k] = taps[t + reach]
    return matrix


def left_weights(matrix):
    high, low = halves(matrix)
    return np.concatenate([high, high, low], axis=1)


def right_weights(*matrices):
    parts = []
    for matrix in matrices:
        parts += list(halves(np.ascontiguousarray(matrix.T)))
    return np.concatenate(parts, axis=1)


def neighbours():
    gx, gy = lax.axis_index("gx"), lax.axis_index("gy")
    nx, ny = lax.axis_size("gx"), lax.axis_size("gy")
    has_x = (gx > 0, gx < nx - 1)
    has_y = (gy > 0, gy < ny - 1)
    at_x = ((gx - 1, gy), (gx + 1, gy))
    at_y = ((gx, gy - 1), (gx, gy + 1))
    return has_x, has_y, at_x, at_y


def greet():
    has_x, has_y, at_x, at_y = neighbours()
    barrier = pltpu.get_barrier_semaphore()
    for has, at in zip(has_x + has_y, at_x + at_y):
        @pl.when(has)
        def _(at=at):
            pl.semaphore_signal(barrier, inc=1, device_id=at, device_id_type=MESH)
    pl.semaphore_wait(barrier, sum(has.astype(jnp.int32) for has in has_x + has_y))


class Exchange:
    def __init__(self, own, ext, hx, hy, cuts, bands, send, recv):
        self.ext, self.hx, self.hy, self.cuts, self.bands = ext, hx, hy, cuts, bands
        self.send, self.recv = send, recv
        self.nx, self.ny = ext.shape[0] - 2 * hx, ext.shape[1] - 2 * hy
        self.own = own
        self.has_x, self.has_y, self.at_x, self.at_y = neighbours()

    @staticmethod
    def count(cuts, bands):
        return 2 * len(bands) + 6 * len(cuts)

    def remote(self, src, dst, index, at):
        return pltpu.make_async_remote_copy(
            src_ref=src, dst_ref=dst, send_sem=self.send.at[index],
            recv_sem=self.recv.at[index], device_id=at, device_id_type=MESH)

    def brick(self, row, rows, col, cols):
        if self.own is None:
            return self.ext.at[pl.ds(self.hx + row, rows), pl.ds(self.hy + col, cols)]
        return self.own.at[pl.ds(row, rows), pl.ds(col, cols)]

    def halo_rows(self, d, cut):
        a, b = cut
        if d == 0:
            return self.nx + self.hx + a, b - a
        return self.hx - b, b - a

    def copy_x(self, d, c):
        a, b = self.cuts[c]
        row, size = self.halo_rows(d, (a, b))
        start = a if d == 0 else self.nx - b
        return self.remote(
            self.brick(start, size, 0, self.ny),
            self.ext.at[pl.ds(row, size), pl.ds(self.hy, self.ny)],
            d * len(self.cuts) + c, self.at_x[d])

    def copy_y(self, d, k):
        a, b = self.bands[k]
        src = 0 if d == 0 else self.ny - self.hy
        dst = self.hy + self.ny if d == 0 else 0
        return self.remote(
            self.brick(a, b - a, src, self.hy),
            self.ext.at[pl.ds(self.hx + a, b - a), pl.ds(dst, self.hy)],
            6 * len(self.cuts) + d * len(self.bands) + k, self.at_y[d])

    def copy_corner(self, side, d, c):
        row, size = self.halo_rows(side, self.cuts[c])
        src = self.hy if d == 0 else self.ny
        dst = self.hy + self.ny if d == 0 else 0
        n = len(self.cuts)
        return self.remote(
            self.ext.at[pl.ds(row, size), pl.ds(src, self.hy)],
            self.ext.at[pl.ds(row, size), pl.ds(dst, self.hy)],
            2 * n + (side * 2 + d) * n + c, self.at_y[d])

    def start_x(self, c):
        for d in range(2):
            pl.when(self.has_x[d])(lambda d=d: self.copy_x(d, c).start())

    def start_y(self, k):
        for d in range(2):
            pl.when(self.has_y[d])(lambda d=d: self.copy_y(d, k).start())

    def clear(self):
        rows, cols, z = self.ext.shape
        for d in range(2):
            @pl.when(jnp.logical_not(self.has_x[d]))
            def _(d=d):
                at = 0 if d == 0 else self.hx + self.nx
                self.ext[pl.ds(at, self.hx)] = jnp.zeros((self.hx, cols, z), F32)

            @pl.when(jnp.logical_not(self.has_y[d]))
            def _(d=d):
                at = 0 if d == 0 else self.hy + self.ny
                self.ext[:, pl.ds(at, self.hy)] = jnp.zeros((rows, self.hy, z), F32)

    def forward(self, c):
        for side in range(2):
            @pl.when(self.has_x[1 - side])
            def _(side=side):
                self.copy_x(side, c).wait_recv()
                for d in range(2):
                    pl.when(self.has_y[d])(lambda d=d: self.copy_corner(side, d, c).start())

    def wait_y(self, k):
        for d in range(2):
            pl.when(self.has_y[1 - d])(lambda d=d: self.copy_y(d, k).wait_recv())

    def wait_corner(self, c):
        for side in range(2):
            for d in range(2):
                pl.when(jnp.logical_and(self.has_x[1 - side], self.has_y[1 - d]))(
                    lambda d=d, side=side: self.copy_corner(side, d, c).wait_recv())

    def wait_sends(self):
        for d in range(2):
            for k in range(len(self.bands)):
                pl.when(self.has_y[d])(lambda d=d, k=k: self.copy_y(d, k).wait_send())
            for c in range(len(self.cuts)):
                pl.when(self.has_x[d])(lambda d=d, c=c: self.copy_x(d, c).wait_send())
                for side in range(2):
                    pl.when(jnp.logical_and(self.has_x[1 - side], self.has_y[d]))(
                        lambda d=d, c=c, side=side: self.copy_corner(side, d, c).wait_send())


def split(value):
    high = value.astype(BF16)
    return high, (value - high.astype(F32)).astype(BF16)


def dot(a, b):
    return jnp.dot(a, b, preferred_element_type=F32)


def left(weights, value):
    high, low = split(value)
    return dot(weights, jnp.concatenate([high, low, high], axis=0))


def right(value, high_w, low_w):
    high, low = split(value)
    return dot(high, high_w) + dot(low, high_w) + dot(high, low_w)


STEP = 5
IMG_CUTS = tuple((a, a + STEP) for a in range(0, IMG_X, STEP))
POT_CUTS = ((0, POT_X),)


def brick_bands(bx):
    middle = bx // 2
    return ((0, POT_X), (bx - POT_X, bx), (POT_X, middle), (middle, bx - POT_X))


def tensor_kernel(image, phases_in, table_in, start, wg_in, ws_in, zg_in, zs_in, cond, pot,
                  ext, masked, along, smooth, phases, table, wg, ws, zg, zs, *sems):
    gx, gy = lax.axis_index("gx"), lax.axis_index("gy")
    bx, by, z = phases.shape
    size_x, size_y = bx * lax.axis_size("gx"), by * lax.axis_size("gy")
    wide_y = ext.shape[1]
    rows_x = bx + 2 * SMOOTH
    bands = brick_bands(bx)

    img = Exchange(image, ext, IMG_X, IMG_Y, IMG_CUTS, ((0, bx),), *sems[0:2])
    pots = Exchange(start, pot, POT_X, POT_Y, POT_CUTS, ((0, bx),), *sems[2:4])
    conds = Exchange(None, cond, POT_X, POT_Y, POT_CUTS, bands, *sems[4:6])
    own_image = pltpu.make_async_copy(
        image, ext.at[pl.ds(IMG_X, bx), pl.ds(IMG_Y, by)], sems[6])
    own_start = pltpu.make_async_copy(
        start, pot.at[pl.ds(POT_X, bx), pl.ds(POT_Y, by)], sems[7])

    loads = [
        pltpu.make_async_copy(src, dst, sems[8 + k])
        for k, (src, dst) in enumerate((
            (wg_in, wg), (zg_in, zg), (ws_in, ws), (phases_in, phases), (zs_in, zs),
            (table_in, table)))
    ]
    own_image.start()
    for load in loads:
        load.start()
    greet()
    img.start_x(0)
    img.start_y(0)
    for c in range(1, len(IMG_CUTS)):
        img.start_x(c)
    own_start.start()
    for part in (img, pots, conds):
        part.clear()

    for load in loads[:3]:
        load.wait()
    row_y = gy * by - IMG_Y + lax.broadcasted_iota(jnp.int32, (wide_y, wg.shape[1]), 0)
    inside = jnp.logical_and(row_y >= 0, row_y < size_y)
    for k in range(2):
        part = wg[k * wide_y:(k + 1) * wide_y].astype(F32)
        masked[k * wide_y:(k + 1) * wide_y] = jnp.where(inside, part, 0.0).astype(BF16)
    own_image.wait()

    def derive(row):
        firsts, seconds = [], []
        for j in range(STEP):
            r = row + j
            at = gx * bx + r - SMOOTH
            ok = jnp.logical_and(at >= 0, at < size_x).astype(F32)
            e = [ext[r + t] for t in range(2 * DERIV + 1)]
            a = e[DERIV] * (NEAR[DERIV] * ok)
            b = jnp.zeros_like(a)
            for t in range(1, DERIV + 1):
                a = a + (e[DERIV + t] + e[DERIV - t]) * (NEAR[DERIV + t] * ok)
                b = b + (e[DERIV + t] - e[DERIV - t]) * (SLOPE[DERIV + t] * ok)
            y_a = left(masked[...], a)
            y_b = left(masked[:wide_y], b)
            firsts += [y_b, y_a[wide_y:]]
            seconds.append(y_a[:wide_y])
        first = right(jnp.concatenate(firsts, axis=0), zg[:, :z], zg[:, z:2 * z])
        second = right(jnp.concatenate(seconds, axis=0), zg[:, 2 * z:3 * z], zg[:, 3 * z:])
        for j in range(STEP):
            r = row + j
            g_x = first[2 * j * wide_y:(2 * j + 1) * wide_y]
            g_y = first[(2 * j + 1) * wide_y:(2 * j + 2) * wide_y]
            g_z = second[j * wide_y:(j + 1) * wide_y]
            for f, (p, q) in enumerate(
                ((g_x, g_x), (g_y, g_y), (g_z, g_z), (g_x, g_y), (g_x, g_z), (g_y, g_z))
            ):
                along[f, r] = left(ws[...], p * q)

    def derive_both(low, high):
        def step(k, carry):
            derive(low + k * (high - low))
            return carry
        lax.fori_loop(0, 2, step, 0)

    centre = rows_x // 2
    img.forward(0)
    img.wait_y(0)
    derive_both(centre - STEP, centre)
    tiles_y, tiles_z = by // 8, z // 128

    def smooth_x(known, ready, add):
        def step(n, carry):
            f = n // (tiles_y * tiles_z)
            ys = pl.ds(pl.multiple_of((n // tiles_z) % tiles_y * 8, 8), 8)
            zz = pl.ds(pl.multiple_of(n % tiles_z * 128, 128), 128)
            new = [r in known and r not in ready for r in range(rows_x)]
            v = [along[f, r, ys, zz] if new[r] else None for r in range(rows_x)]
            for i in range(bx):
                c = i + SMOOTH
                terms = [v[c] * WIDE[SMOOTH]] if new[c] else []
                for t in range(1, SMOOTH + 1):
                    pair = [v[r] for r in (c + t, c - t) if new[r]]
                    if pair:
                        terms.append((pair[0] + pair[1] if len(pair) > 1 else pair[0])
                                     * WIDE[SMOOTH + t])
                if terms:
                    total = smooth[f, i, ys, zz] if add else terms.pop(0)
                    for term in terms:
                        total = total + term
                    smooth[f, i, ys, zz] = total
            return carry
        lax.fori_loop(0, 6 * tiles_y * tiles_z, step, 0)

    last = len(IMG_CUTS) - 1
    for c in range(last):
        img.forward(c + 1)
        img.wait_corner(c)
        derive_both(centre - (c + 2) * STEP, centre + (c + 1) * STEP)
    pots.start_x(0)
    pots.start_y(0)
    inner = range(STEP, rows_x - STEP)
    smooth_x(inner, (), False)
    img.wait_corner(last)
    derive_both(0, rows_x - STEP)
    pots.forward(0)
    smooth_x(range(rows_x), inner, True)
    for load in loads[3:]:
        load.wait()

    def finish(rows):
        every = right(
            jnp.concatenate([smooth[f, i] for i in rows for f in range(6)], axis=0),
            zs[:, :z], zs[:, z:])
        for n, i in enumerate(rows):
            s = every[n * 6 * by:(n + 1) * 6 * by]
            jxx, jyy, jzz, jxy, jxz, jyz = (s[f * by:(f + 1) * by] for f in range(6))
            trace = jxx + jyy + jzz
            shift = 0.1 * trace + 1e-06
            a, b, c = jxx + shift, jyy + shift, jzz + shift
            cof = a * b - jxy * jxy
            det = (
                a * (b * c - jyz * jyz)
                - jxy * (jxy * c - jyz * jxz)
                + jxz * (jxy * jyz - b * jxz)
            )
            weight = trace * cof / det
            label = phases[i]
            base = jnp.where(
                label == 0, table[0, 0], jnp.where(label == 1, table[0, 1], table[0, 2]))
            aniso = jnp.where(
                label == 0, table[1, 0], jnp.where(label == 1, table[1, 1], table[1, 2]))
            cond[POT_X + i, POT_Y:POT_Y + by] = base + 0.1 * aniso * weight

    finish([i for low, high in bands[:2] for i in range(low, high)])
    conds.start_x(0)
    conds.start_y(0)
    conds.start_y(1)
    for k in range(2, len(bands)):
        finish(list(range(*bands[k])))
        conds.start_y(k)
    conds.forward(0)

    own_start.wait()
    pots.wait_y(0)
    pots.wait_corner(0)
    for k in range(len(bands)):
        conds.wait_y(k)
    conds.wait_corner(0)
    for part in (img, pots, conds):
        part.wait_sends()


def tensor(image, phases, table, start):
    bx, by, z = phases.shape
    wide_y = by + 2 * IMG_Y
    rows_x = bx + 2 * SMOOTH
    lo, hi = IMG_Y - SMOOTH, wide_y - (IMG_Y - SMOOTH)
    wg = np.concatenate([
        left_weights(band(wide_y, wide_y, 0, NEAR, lo, hi)),
        left_weights(band(wide_y, wide_y, 0, SLOPE, lo, hi)),
    ], axis=0)
    ws = left_weights(band(by, wide_y, IMG_Y, WIDE))
    zg = right_weights(band(z, z, 0, NEAR), band(z, z, 0, SLOPE))
    zs = right_weights(band(z, z, 0, WIDE))
    vmem = pl.BlockSpec(memory_space=pltpu.VMEM)
    anywhere = pl.BlockSpec(memory_space=pl.ANY)
    outer = jax.ShapeDtypeStruct((bx + 2 * POT_X, by + 2 * POT_Y, z), F32)
    sems = []
    for count in (
        Exchange.count(IMG_CUTS, ((0, bx),)),
        Exchange.count(POT_CUTS, ((0, bx),)),
        Exchange.count(POT_CUTS, brick_bands(bx)),
    ):
        sems += [pltpu.SemaphoreType.DMA((count,))] * 2
    return pl.pallas_call(
        tensor_kernel,
        out_shape=[outer, outer],
        in_specs=[anywhere] * 8,
        out_specs=[vmem, vmem],
        scratch_shapes=[
            pltpu.VMEM((bx + 2 * IMG_X, wide_y, z), F32),
            pltpu.VMEM(wg.shape, BF16),
            pltpu.VMEM((6, rows_x, by, z), F32),
            pltpu.VMEM((6, bx, by, z), F32),
            pltpu.VMEM(phases.shape, jnp.int32),
            pltpu.SMEM(table.shape, F32),
        ] + [pltpu.VMEM(w.shape, BF16) for w in (wg, ws, zg, zs)]
        + sems + [pltpu.SemaphoreType.DMA] * 8,
        compiler_params=pltpu.CompilerParams(
            collective_id=0, has_side_effects=True, vmem_limit_bytes=VMEM_LIMIT),
    )(image, phases, table, start, wg, ws, zg, zs)


def harmonic(p, q):
    total = p + q
    return 2.0 * p * q / jnp.where(total > 0, total, 1.0)


def step_of(count):
    return max(n for n in (1, 2, 3, 4) if count % n == 0)


def sweep_kernel(cond_in, start_in, centre, out, cond, start, kx, y0, y1, z0, z1, inv, one, two,
                 *sems):
    rows, wide, z = cond.shape
    get_cond = pltpu.make_async_copy(cond_in, cond, sems[0])
    get_start = pltpu.make_async_copy(start_in, start, sems[1])
    get_cond.start()
    get_start.start()
    get_cond.wait()
    copy = pltpu.make_async_copy(
        cond.at[pl.ds(POT_X, rows - 2 * POT_X), pl.ds(POT_Y, wide - 2 * POT_Y)], centre, sems[2])
    copy.start()
    lane = lax.broadcasted_iota(jnp.int32, (1, wide, z), 2)
    at_low, at_high = lane == 0, lane == z - 1

    def roll_y(v, s):
        return pltpu.roll(v, s % wide, 1)

    def roll_z(v, s):
        return pltpu.roll(v, s % z, 2)

    kx[0] = harmonic(cond[0], cond[1])
    size = 2

    def coefficients(step, carry):
        j = 1 + step * size
        c = cond[pl.ds(j, size)]
        x_up = harmonic(c, cond[pl.ds(j + 1, size)])
        y_up = harmonic(c, roll_y(c, -1))
        z_up = harmonic(c, roll_z(c, -1))
        x_down = jnp.concatenate([kx[j - 1][None], x_up[:size - 1]], axis=0)
        y_down = roll_y(y_up, 1)
        low = jnp.where(at_low, c, roll_z(z_up, 1))
        high = jnp.where(at_high, c, z_up)
        total = x_down + x_up + y_down + y_up + low + high
        kx[pl.ds(j, size)] = x_up
        y0[pl.ds(j, size)] = y_down
        y1[pl.ds(j, size)] = y_up
        z0[pl.ds(j, size)] = low
        z1[pl.ds(j, size)] = high
        inv[pl.ds(j, size)] = 1.0 / jnp.where(total > 0, total, 1.0)
        return carry

    lax.fori_loop(0, (rows - 2) // size, coefficients, 0)
    get_start.wait()

    def sweep(src, dst, shift, cols, first, last):
        size = step_of(last - first)

        def step(k, carry):
            j = first + k * size
            at = pl.ds(j, size)
            p = src[at]
            numer = kx[pl.ds(j - 1, size)] * src[pl.ds(j - 1, size)]
            numer = numer + kx[at] * src[pl.ds(j + 1, size)]
            numer = numer + y0[at] * roll_y(p, 1) + y1[at] * roll_y(p, -1)
            numer = numer + z0[at] * jnp.where(at_low, 1.0, roll_z(p, 1))
            numer = numer + z1[at] * jnp.where(at_high, 0.0, roll_z(p, -1))
            value = numer * inv[at]
            dst[pl.ds(j - shift, size)] = value[:, cols:wide - cols]
            return carry
        lax.fori_loop(0, (last - first) // size, step, 0)

    sweep(start, one, 0, 0, 1, rows - 1)
    sweep(one, two, 0, 0, 2, rows - 2)
    sweep(two, out, POT_X, POT_Y, 3, rows - 3)
    copy.wait()


def sweeps(cond_ext, pot_ext):
    rows, wide, z = cond_ext.shape
    vmem = pl.BlockSpec(memory_space=pltpu.VMEM)
    brick = jax.ShapeDtypeStruct((rows - 2 * POT_X, wide - 2 * POT_Y, z), F32)
    return pl.pallas_call(
        sweep_kernel,
        out_shape=[brick, brick],
        in_specs=[pl.BlockSpec(memory_space=pl.ANY)] * 2,
        out_specs=[pl.BlockSpec(memory_space=pl.ANY), vmem],
        scratch_shapes=[pltpu.VMEM((rows, wide, z), F32)] * 10 + [pltpu.SemaphoreType.DMA] * 3,
        compiler_params=pltpu.CompilerParams(vmem_limit_bytes=VMEM_LIMIT),
    )(cond_ext, pot_ext)


def body(image, phases, phase_table, start_potential):
    cond_ext, pot_ext = tensor(image, phases, phase_table, start_potential)
    conductivity, potential = sweeps(cond_ext, pot_ext)
    return conductivity, potential


def solution(mesh):
    placed = (P("gx", "gy", None), P("gx", "gy", None), P(), P("gx", "gy", None))
    return jax.shard_map(
        body,
        mesh=mesh,
        in_specs=placed,
        out_specs=(P("gx", "gy", None), P("gx", "gy", None)),
        check_vma=False,
    )
```
